256 devices in a mesh: seq: 64 (over z, y, core), sp: 4 (over x).
Axes of the slice: x: 4, y: 4, z: 8, core: 2. Of those that a mesh axis runs over, the one named last changes fastest.
Arguments:
- frames_in: bfloat16 [384, 32, 32, 384], P('seq', 'sp'), may hold values from -6 to 6
- gain: float32 [384], replicated, may hold values from 0.1 to 1.9
- conv_weight: bfloat16 [3, 3, 3, 384, 384], replicated, may hold values from -0.0625 to 0.0625
- conv_bias: float32 [384], replicated, may hold values from -3 to 3
- time_weight: bfloat16 [3, 384, 384], replicated, may hold values from -0.1875 to 0.1875
- time_bias: float32 [384], replicated, may hold values from -3 to 3
- clip_lengths: int32 [16], replicated, may hold values from 1 to 6, 64 in all
Outputs:
- latent: bfloat16 [192, 32, 32, 384], P('seq', 'sp')
The draws below stay inside these ranges and needn't reach their ends.
Inputs may be any that keep to these rules, and one draw needn't show every extreme that they name: `clip_lengths`: the clips cover the 64 groups in order; the longest clip has exactly 6 groups.
All inputs are finite; a program needn't handle non-finite values.
Results may differ from the reference program's by a relative error of at most 0.005.
Values may be sent and summed in bfloat16 or wider, within the bound.
A program may use at most 128 MiB of HBM per device.

```python
import math
import jax
import jax.numpy as jnp
import numpy as np
from jax import lax

C = 384
COLS = 32
FRAMES = 6
MOST = 6
GROUPS = 64
CLIPS = 16
NF = 384
HEIGHT = 32


def shard_levels(own_key, dims, shards, low, top_value):
    level = 1.0
    for position, blocks in shards:
        heights = jax.random.uniform(jax.random.fold_in(jax.random.fold_in(own_key, 6), position), (blocks,), jnp.float32, low / len(shards), top_value / len(shards))
        level = level * jnp.repeat(jnp.exp(heights), dims[position] // blocks).reshape((-1,) + (1,) * (len(dims) - 1 - position))
    return level


def profile(number_of, total, most, slope):
    weights = [(1 << 20) // math.isqrt(standing ** slope) + 1 for standing in range(2, number_of + 1)]
    spare, holding = total - most - (number_of - 1), [1] * (number_of - 1)
    while spare > 0:
        movable = [i for i in range(number_of - 1) if holding[i] < most]
        mass, budget = sum([weights[i] for i in movable]), spare
        for i in movable:
            more = min(most - holding[i], max(1, budget * weights[i] // mass), spare)
            holding[i] = holding[i] + more
            spare = spare - more
    return np.array([most] + holding)


def uneven(key, amount, total, most, lean):
    if amount == 2:
        one = jax.random.randint(key, (), max(1, total - most), min(most, total - 1) + 1)
        return jnp.stack([one, total - one])
    lengths = jnp.asarray(profile(amount, total, most, lean), jnp.int32)
    twos = (amount - 1) // 2
    source_of, taker = lengths[1:1 + 2 * twos:2], lengths[2:2 + 2 * twos:2]
    room = jnp.minimum(source_of - 1, most - taker)
    moved = jax.random.randint(jax.random.fold_in(key, 1), (twos,), 0, 1 << 20) % (room + 1)
    lengths = lengths.at[1:1 + 2 * twos:2].set(source_of - moved).at[2:2 + 2 * twos:2].set(taker + moved)
    return lengths[jax.random.permutation(jax.random.fold_in(key, 2), amount)]


def noise(own_key, extent, spread, most, split=(), kind=jnp.bfloat16):
    loudness = shard_levels(own_key, extent, split, -0.22, 0.18) if split else 1.0
    result = jax.random.normal(own_key, extent, jnp.float32) * spread * loudness
    return jnp.minimum(jnp.maximum(result, -most), most).astype(kind)


def setup_inputs(seed: int = 0) -> dict:
    keys = jax.random.split(jax.random.key(seed), 8)
    return {
        "frames_in": noise(keys[0], (NF, HEIGHT, COLS, C), 1.0, 6.0, ((0, 64), (1, 4))),
        "gain": jnp.clip(1.0 + 0.18 * jax.random.normal(keys[1], (C,), jnp.float32), 0.1, 1.9),
        "conv_weight": noise(keys[2], (3, 3, 3, C, C), (27 * C) ** -0.5, 0.0625),
        "conv_bias": noise(keys[3], (C,), 0.5, 3.0, (), jnp.float32),
        "time_weight": noise(keys[4], (3, C, C), (3 * C) ** -0.5, 0.1875),
        "time_bias": noise(keys[5], (C,), 0.5, 3.0, (), jnp.float32),
        "clip_lengths": uneven(keys[6], CLIPS, GROUPS, MOST, 2).astype(jnp.int32),
    }


def normalize(values, gain):
    scale = lax.rsqrt(lax.optimization_barrier(jnp.mean(values * values, axis=-1, keepdims=True)) + 1e-06)
    return jax.nn.silu(values * scale * gain).astype(jnp.bfloat16)

def reference(frames_in, gain, conv_weight, conv_bias, time_weight, time_bias, clip_lengths):
    x_float = frames_in.astype(jnp.float32)
    act = normalize(x_float, gain).astype(jnp.float32)
    total = frames_in.shape[0]
    starts = (jnp.cumsum(clip_lengths) - clip_lengths).astype(jnp.int32)
    frame = jnp.arange(total, dtype=jnp.int32)
    group = frame // FRAMES
    first_group = lax.optimization_barrier(jnp.max(jnp.where(starts[None, :] <= group[:, None], starts[None, :], 0), axis=1))
    first_frame = (first_group * FRAMES).astype(jnp.int32)
    accum = jnp.zeros(frames_in.shape, jnp.float32)
    for lag in range(3):
        shifted = jnp.concatenate([jnp.zeros((lag,) + act.shape[1:], jnp.float32), act[:total - lag]], 0)
        valid = frame - lag >= first_frame
        shifted = jnp.where(valid[:, None, None, None], shifted, 0.0)
        kernel = conv_weight[2 - lag].astype(jnp.float32)
        accum = accum + lax.conv_general_dilated(shifted, kernel, (1, 1), ((1, 1), (1, 1)), dimension_numbers=('NHWC', 'HWIO', 'NHWC'), precision=lax.Precision.HIGHEST)
    resid = (x_float + accum + conv_bias).astype(jnp.bfloat16)
    y_float = resid.astype(jnp.float32)
    earlier = jnp.concatenate([jnp.zeros((1,) + y_float.shape[1:], jnp.float32), y_float[:-1]], 0)
    earlier = jnp.where((frame - 1 >= first_frame)[:, None, None, None], earlier, 0.0)
    width = frames_in.shape[-1]

    def project(values, weight):
        flat = jnp.dot(values.reshape(-1, width), weight.astype(jnp.float32), precision=lax.Precision.HIGHEST)
        return flat.reshape(values.shape)
    latent = project(earlier[0::2], time_weight[0]) + project(y_float[0::2], time_weight[1]) + project(y_float[1::2], time_weight[2]) + time_bias
    return latent.astype(jnp.bfloat16)
```

```python
import jax
import jax.numpy as jnp
from jax import lax
from jax.experimental import pallas as pl
from jax.experimental.pallas import tpu as pltpu
from jax.sharding import PartitionSpec as P

F32 = jnp.float32
BF16 = jnp.bfloat16
MESH = pl.DeviceIdType.MESH
TAPS = 3


def kernel(
    x_ref, gain_ref, cw_ref, cb_ref, tw_ref, tb_ref, clips_ref, out_ref,
    x_all, weight, time_w, vectors, joined, total, resid, before, latent,
    x_sem, w_sem, small_sem, send_sem, recv_sem, out_sem,
):
    frames, rows, cols, width = x_ref.shape
    lag = TAPS - 1
    seq_count, sp_count = lax.axis_size("seq"), lax.axis_size("sp")
    seq, sp = lax.axis_index("seq"), lax.axis_index("sp")
    seq_next, seq_back = lax.rem(seq + 1, seq_count), lax.rem(seq + seq_count - 1, seq_count)
    sp_next, sp_back = lax.rem(sp + 1, sp_count), lax.rem(sp + sp_count - 1, sp_count)

    loads = []
    for t in range(frames):
        loads.append(
            pltpu.make_async_copy(x_ref.at[t], x_all.at[lag + t, pl.ds(1, rows)], x_sem.at[t])
        )
    small = [
        pltpu.make_async_copy(source, vectors.at[pl.ds(8 * i, 1)], small_sem.at[i])
        for i, source in enumerate((gain_ref, cb_ref, tb_ref))
    ]
    weights = [
        pltpu.make_async_copy(
            cw_ref.at[k], weight.at[:, pl.ds(k * width, width)], w_sem.at[k]
        )
        for k in range(TAPS)
    ]
    time_load = pltpu.make_async_copy(tw_ref, time_w, w_sem.at[TAPS])
    small[0].start()
    for t in reversed(range(frames)):
        loads[t].start()
    for k in reversed(range(TAPS)):
        weights[k].start()
    time_load.start()
    small[1].start()
    small[2].start()

    barrier = pltpu.get_barrier_semaphore()
    for device in (
        (seq, sp_next), (seq, sp_back), (seq_back, sp), (seq_back, sp_next), (seq_back, sp_back)
    ):
        pl.semaphore_signal(barrier, inc=1, device_id=device, device_id_type=MESH)
    pl.semaphore_wait(barrier, 5)

    def send(slot, source, target, device):
        copy = pltpu.make_async_remote_copy(
            src_ref=source, dst_ref=target, send_sem=send_sem.at[slot], recv_sem=recv_sem.at[slot],
            device_id=device, device_id_type=MESH,
        )
        copy.start()
        return copy

    last = pl.ds(frames - lag, lag)
    own, past = pl.ds(lag, frames), pl.ds(0, lag)
    above = send(0, x_ref.at[:, rows - 1], x_all.at[own, 0], (seq, sp_next))
    below = send(1, x_ref.at[:, 0], x_all.at[own, rows + 1], (seq, sp_back))
    earlier = [
        send(2, x_ref.at[last], x_all.at[past, pl.ds(1, rows)], (seq_next, sp)),
        send(3, x_ref.at[last, rows - 1], x_all.at[past, 0], (seq_next, sp_next)),
        send(4, x_ref.at[last, 0], x_all.at[past, rows + 1], (seq_next, sp_back)),
    ]

    opening = jnp.int32(0)
    start = jnp.int32(0)
    for j in range(clips_ref.shape[0]):
        opening = opening + jnp.where(start == seq, 1, 0)
        start = start + clips_ref[j]
    keep = (1 - opening).astype(F32)
    has_above = jnp.where(sp > 0, 1, 0).astype(F32)
    has_below = jnp.where(sp < sp_count - 1, 1, 0).astype(F32)

    small[0].wait()
    half_gain = vectors[0:1] * 0.5
    column = lax.broadcasted_iota(jnp.int32, (cols, width), 0)

    def normalize(s, r, factor):
        values = x_all[s, r].astype(F32)
        scale = lax.rsqrt(jnp.mean(values * values, axis=-1, keepdims=True) + 1e-06)
        if factor is not None:
            scale = scale * factor
        half = values * scale * half_gain
        act = half + half * jnp.tanh(half)
        joined[s, r, :, pl.ds(width, width)] = act.astype(BF16)
        ahead = jnp.where(column == 0, 0.0, pltpu.roll(act, 1, 0))
        joined[s, r, :, pl.ds(0, width)] = ahead.astype(BF16)
        behind = jnp.where(column == cols - 1, 0.0, pltpu.roll(act, cols - 1, 0))
        joined[s, r, :, pl.ds(2 * width, width)] = behind.astype(BF16)

    def conv(s):
        left = jnp.concatenate(
            [joined[s, d : d + rows].reshape(rows * cols, TAPS * width) for d in range(TAPS)], 1
        )
        taps = [k for k in range(TAPS) if 0 <= s - k < frames]
        part = jnp.dot(
            left, weight[:, taps[0] * width : (taps[-1] + 1) * width], preferred_element_type=F32
        )
        for n, k in enumerate(taps):
            t = s - k
            piece = part[:, n * width : (n + 1) * width]
            if k == TAPS - 1 or s == frames + lag - 1:
                total[t] = piece
            elif k == 0:
                finish(t, total[t] + piece)
            else:
                total[t] = total[t] + piece

    def finish(t, summed):
        values = x_all[lag + t, 1 : rows + 1].reshape(rows * cols, width).astype(F32)
        resid[t + 1] = (values + summed + vectors[8:9]).astype(BF16)

    def project(j):
        left = jnp.concatenate([resid[2 * j + k] for k in range(TAPS)], 1)
        done = jnp.dot(left, time_w[...], preferred_element_type=F32) + vectors[16:17]
        latent[j] = done.reshape(rows, cols, width).astype(BF16)
        copy = pltpu.make_async_copy(latent.at[j], out_ref.at[j], out_sem.at[j])
        copy.start()
        return copy

    for t in reversed(range(frames)):
        loads[t].wait()
        for r in range(1, rows + 1):
            normalize(lag + t, r, None)
    above.wait_recv()
    below.wait_recv()
    for t in reversed(range(frames)):
        normalize(lag + t, 0, has_above)
        normalize(lag + t, rows + 1, has_below)
    small[1].wait()
    small[2].wait()
    weights[2].wait()
    conv(7)
    weights[1].wait()
    conv(6)
    weights[0].wait()
    conv(5)
    before_copy = send(5, resid.at[frames], before, (seq_next, sp))
    conv(4)
    conv(3)
    time_load.wait()
    outs = [project(2)]
    conv(2)
    for copy in earlier:
        copy.wait_recv()
    for s in reversed(range(lag)):
        normalize(s, 0, has_above * keep)
        for r in range(1, rows + 1):
            normalize(s, r, keep)
        normalize(s, rows + 1, has_below * keep)
    conv(1)
    outs.append(project(1))
    conv(0)
    before_copy.wait_recv()
    resid[0] = (before[...].astype(F32) * keep).astype(BF16)
    outs.append(project(0))
    for copy in [above, below, *earlier, before_copy]:
        copy.wait_send()
    for copy in outs:
        copy.wait()


def per_device(frames_in, gain, conv_weight, conv_bias, time_weight, time_bias, clip_lengths):
    frames, rows, cols, width = frames_in.shape
    deep = TAPS * TAPS * width
    lag = TAPS - 1
    anywhere = pl.BlockSpec(memory_space=pl.ANY)
    flops = 2 * frames * rows * cols * width * (TAPS * deep + TAPS * width // 2)
    return pl.pallas_call(
        kernel,
        out_shape=jax.ShapeDtypeStruct((frames // 2, rows, cols, width), BF16),
        in_specs=[anywhere] * 6 + [pl.BlockSpec(memory_space=pltpu.SMEM)],
        out_specs=anywhere,
        scratch_shapes=[
            pltpu.VMEM((frames + lag, rows + 2, cols, width), BF16),
            pltpu.VMEM((deep, TAPS * width), BF16),
            pltpu.VMEM((TAPS * width, width), BF16),
            pltpu.VMEM((24, width), F32),
            pltpu.VMEM((frames + lag, rows + 2, cols, TAPS * width), BF16),
            pltpu.VMEM((frames, rows * cols, width), F32),
            pltpu.VMEM((frames + 1, rows * cols, width), BF16),
            pltpu.VMEM((rows * cols, width), BF16),
            pltpu.VMEM((frames // 2, rows, cols, width), BF16),
            pltpu.SemaphoreType.DMA((frames,)),
            pltpu.SemaphoreType.DMA((TAPS + 1,)),
            pltpu.SemaphoreType.DMA((3,)),
            pltpu.SemaphoreType.DMA((6,)),
            pltpu.SemaphoreType.DMA((6,)),
            pltpu.SemaphoreType.DMA((frames // 2,)),
        ],
        compiler_params=pltpu.CompilerParams(
            collective_id=0, has_side_effects=True, vmem_limit_bytes=56 * 2**20
        ),
        cost_estimate=pl.CostEstimate(flops=flops, bytes_accessed=12_000_000, transcendentals=0),
        name="residual_block",
    )(
        frames_in,
        gain.reshape(1, width),
        conv_weight.reshape(TAPS, deep, width),
        conv_bias.reshape(1, width),
        time_weight.reshape(TAPS * width, width),
        time_bias.reshape(1, width),
        clip_lengths,
    )


def solution(mesh):
    return jax.shard_map(
        per_device,
        mesh=mesh,
        in_specs=(P("seq", "sp", None, None), P(), P(), P(), P(), P(), P()),
        out_specs=P("seq", "sp", None, None),
        check_vma=False,
    )
```

```python
import jax
import jax.numpy as jnp
from jax import lax
from jax.experimental import pallas as pl
from jax.experimental.pallas import tpu as pltpu
from jax.sharding import PartitionSpec as P

F32 = jnp.float32
BF16 = jnp.bfloat16
MESH = pl.DeviceIdType.MESH
TAPS = 3


def kernel(
    x_ref, gain_ref, cw_ref, cb_ref, tw_ref, tb_ref, clips_ref, out_ref,
    x_all, weight, time_w, gain_v, cb_v, tb_v, joined, total, resid, before, latent,
    x_sem, w_sem, small_sem, send_sem, recv_sem, out_sem,
):
    frames, rows, cols, width = x_ref.shape
    lag = TAPS - 1
    deep = TAPS * width
    seq_count, sp_count = lax.axis_size("seq"), lax.axis_size("sp")
    seq, sp = lax.axis_index("seq"), lax.axis_index("sp")
    seq_next, seq_back = lax.rem(seq + 1, seq_count), lax.rem(seq + seq_count - 1, seq_count)
    sp_next, sp_back = lax.rem(sp + 1, sp_count), lax.rem(sp + sp_count - 1, sp_count)

    barrier = pltpu.get_barrier_semaphore()
    for device in (
        (seq, sp_next), (seq, sp_back), (seq_back, sp), (seq_back, sp_next), (seq_back, sp_back)
    ):
        pl.semaphore_signal(barrier, inc=1, device_id=device, device_id_type=MESH)

    small = [
        pltpu.make_async_copy(source, target, small_sem.at[i])
        for i, (source, target) in enumerate(((gain_ref, gain_v), (cb_ref, cb_v), (tb_ref, tb_v)))
    ]
    loads = [
        pltpu.make_async_copy(x_ref.at[t], x_all.at[lag + t, pl.ds(1, rows)], x_sem.at[t])
        for t in range(frames)
    ]

    def weight_load(slot, first, size):
        return [
            pltpu.make_async_copy(
                cw_ref.at[k, pl.ds(first, size)],
                weight.at[pl.ds(first, size), pl.ds(k * width, width)],
                w_sem.at[slot + k],
            )
            for k in range(TAPS)
        ]

    head, tail = weight_load(0, 0, deep), weight_load(TAPS, deep, 2 * deep)
    time_load = pltpu.make_async_copy(tw_ref, time_w, w_sem.at[2 * TAPS])
    small[0].start()
    for t in (3, 2, 1, 5, 4, 0):
        loads[t].start()
    for copy in head:
        copy.start()

    pl.semaphore_wait(barrier, 5)

    def send(slot, source, target, device):
        copy = pltpu.make_async_remote_copy(
            src_ref=source, dst_ref=target, send_sem=send_sem.at[slot], recv_sem=recv_sem.at[slot],
            device_id=device, device_id_type=MESH,
        )
        copy.start()
        return copy

    last = pl.ds(frames - lag, lag)
    own, past = pl.ds(lag, frames), pl.ds(0, lag)
    above = send(0, x_ref.at[:, rows - 1], x_all.at[own, 0], (seq, sp_next))
    below = send(1, x_ref.at[:, 0], x_all.at[own, rows + 1], (seq, sp_back))
    earlier = [
        send(2, x_ref.at[last], x_all.at[past, pl.ds(1, rows)], (seq_next, sp)),
        send(3, x_ref.at[last, rows - 1], x_all.at[past, 0], (seq_next, sp_next)),
        send(4, x_ref.at[last, 0], x_all.at[past, rows + 1], (seq_next, sp_back)),
    ]

    opening = jnp.int32(0)
    start = jnp.int32(0)
    for j in range(clips_ref.shape[0]):
        opening = opening + jnp.where(start == seq, 1, 0)
        start = start + clips_ref[j]
    keep = (1 - opening).astype(F32)
    has_above = jnp.where(sp > 0, 1, 0).astype(F32)
    has_below = jnp.where(sp < sp_count - 1, 1, 0).astype(F32)

    small[0].wait()
    half_gain = gain_v[...].reshape(1, width) * 0.5
    column = lax.broadcasted_iota(jnp.int32, (cols, width), 0)

    def normalize(s, r, factor=None):
        values = x_all[s, r].astype(F32)
        scale = lax.rsqrt(jnp.mean(values * values, axis=-1, keepdims=True) + 1e-06)
        if factor is not None:
            scale = scale * factor
        half = values * scale * half_gain
        act = half + half * jnp.tanh(half)
        joined[s, r, :, pl.ds(width, width)] = act.astype(BF16)
        ahead = jnp.where(column == 0, 0.0, pltpu.roll(act, 1, 0))
        joined[s, r, :, pl.ds(0, width)] = ahead.astype(BF16)
        behind = jnp.where(column == cols - 1, 0.0, pltpu.roll(act, cols - 1, 0))
        joined[s, r, :, pl.ds(2 * width, width)] = behind.astype(BF16)

    queue = []

    def beside(count):
        for _ in range(min(count, len(queue))):
            normalize(*queue.pop(0))

    seen = set()
    inner, edge, whole = (1, rows - 1), None, (0, rows)

    def rows_of(s, part, d):
        if part is edge:
            pair = [joined[s, d], joined[s, rows - 1 + d]]
            return jnp.concatenate(pair, 0)
        lo, hi = part
        return joined[s, lo + d : hi + d].reshape((hi - lo) * cols, deep)

    def conv(sources, part, first=0, count=TAPS, final=()):
        left = jnp.concatenate(
            [
                jnp.concatenate([rows_of(s, part, d) for s in sources], 0)
                for d in range(first, first + count)
            ],
            1,
        )
        taps = [k for k in range(TAPS) if 0 <= sources[0] - k < frames]
        product = jnp.dot(
            left,
            weight[first * deep : (first + count) * deep, taps[0] * width : (taps[-1] + 1) * width],
            preferred_element_type=F32,
        )
        size = left.shape[0] // len(sources)
        sums = {}
        for i, s in enumerate(sources):
            for n, k in enumerate(taps):
                piece = product[i * size : (i + 1) * size, n * width : (n + 1) * width]
                sums[s - k] = sums[s - k] + piece if s - k in sums else piece
        for t, piece in sums.items():
            spots = [0, rows - 1] if part is edge else [slice(*part)]
            for i, spot in enumerate(spots):
                share = piece.shape[0] // len(spots)
                value = piece[i * share : (i + 1) * share]
                value = value.reshape(((share // cols,) if part is not edge else ()) + (cols, width))
                marks = [(t, r) for r in (range(*part) if part is not edge else [spot])]
                if marks[0] in seen:
                    value = total[t, spot] + value
                seen.update(marks)
                if t in final:
                    finish(t, value)
                else:
                    total[t, spot] = value

    def finish(t, summed):
        values = x_all[lag + t, 1 : rows + 1].astype(F32)
        done = values + summed + cb_v[...].reshape(1, 1, width)
        resid[t + 1] = done.reshape(rows * cols, width).astype(BF16)

    def project(j):
        left = jnp.concatenate([resid[2 * j + k] for k in range(TAPS)], 1)
        done = jnp.dot(left, time_w[...], preferred_element_type=F32) + tb_v[...].reshape(1, width)
        latent[j] = done.reshape(rows, cols, width).astype(BF16)
        copy = pltpu.make_async_copy(latent.at[j], out_ref.at[j], out_sem.at[j])
        copy.start()
        return copy

    for t in (3, 2, 1):
        loads[t].wait()
    for copy in tail + [time_load] + small[1:]:
        copy.start()
    for t in (3, 2, 1):
        for r in range(1, rows + 1):
            normalize(lag + t, r)
    for t in (5, 4, 0):
        loads[t].wait()
        queue.extend((lag + t, r) for r in range(1, rows + 1))
    for copy in head:
        copy.wait()
    for s in (5, 4, 3):
        conv((s,), inner, 0, 1)
        beside(4)
    for copy in tail + small[1:]:
        copy.wait()
    for s in (5, 4):
        conv((s,), inner, 1, 2)
        beside(6)
    above.wait_recv()
    below.wait_recv()
    for s in (5, 4, 3):
        normalize(s, 0, has_above)
        normalize(s, rows + 1, has_below)
    for s in (7, 6, 2):
        queue.append((s, 0, has_above))
        queue.append((s, rows + 1, has_below))
    conv((3,), inner, 1, 2)
    conv((5, 4, 3), edge)
    beside(len(queue))
    finish(3, total[3])
    conv((7,), whole)
    conv((6,), whole, final=(5, 4))
    before_copy = send(5, resid.at[frames], before, (seq_next, sp))
    time_load.wait()
    outs = [project(2)]
    for copy in earlier:
        copy.wait_recv()
    for s in reversed(range(lag)):
        normalize(s, 0, has_above * keep)
        for r in range(1, rows + 1):
            normalize(s, r, keep)
        normalize(s, rows + 1, has_below * keep)
    conv((2,), whole, final=(2,))
    conv((1,), whole, final=(1,))
    outs.append(project(1))
    conv((0,), whole, final=(0,))
    before_copy.wait_recv()
    resid[0] = (before[...].astype(F32) * keep).astype(BF16)
    outs.append(project(0))
    for copy in [above, below, *earlier, before_copy]:
        copy.wait_send()
    for copy in outs:
        copy.wait()


def per_device(frames_in, gain, conv_weight, conv_bias, time_weight, time_bias, clip_lengths):
    frames, rows, cols, width = frames_in.shape
    deep = TAPS * TAPS * width
    lag = TAPS - 1
    anywhere = pl.BlockSpec(memory_space=pl.ANY)
    flops = 2 * frames * rows * cols * width * (TAPS * deep + TAPS * width // 2)
    return pl.pallas_call(
        kernel,
        out_shape=jax.ShapeDtypeStruct((frames // 2, rows, cols, width), BF16),
        in_specs=[anywhere] * 6 + [pl.BlockSpec(memory_space=pltpu.SMEM)],
        out_specs=anywhere,
        scratch_shapes=[
            pltpu.VMEM((frames + lag, rows + 2, cols, width), BF16),
            pltpu.VMEM((deep, TAPS * width), BF16),
            pltpu.VMEM((TAPS * width, width), BF16),
            pltpu.VMEM((width,), F32),
            pltpu.VMEM((width,), F32),
            pltpu.VMEM((width,), F32),
            pltpu.VMEM((frames + lag, rows + 2, cols, TAPS * width), BF16),
            pltpu.VMEM((frames, rows, cols, width), F32),
            pltpu.VMEM((frames + 1, rows * cols, width), BF16),
            pltpu.VMEM((rows * cols, width), BF16),
            pltpu.VMEM((frames // 2, rows, cols, width), BF16),
            pltpu.SemaphoreType.DMA((frames,)),
            pltpu.SemaphoreType.DMA((2 * TAPS + 1,)),
            pltpu.SemaphoreType.DMA((3,)),
            pltpu.SemaphoreType.DMA((6,)),
            pltpu.SemaphoreType.DMA((6,)),
            pltpu.SemaphoreType.DMA((frames // 2,)),
        ],
        compiler_params=pltpu.CompilerParams(
            collective_id=0, has_side_effects=True, vmem_limit_bytes=56 * 2**20
        ),
        cost_estimate=pl.CostEstimate(flops=flops, bytes_accessed=12_000_000, transcendentals=0),
        name="residual_block",
    )(
        frames_in,
        gain,
        conv_weight.reshape(TAPS, deep, width),
        conv_bias,
        time_weight.reshape(TAPS * width, width),
        time_bias,
        clip_lengths,
    )


def solution(mesh):
    return jax.shard_map(
        per_device,
        mesh=mesh,
        in_specs=(P("seq", "sp", None, None), P(), P(), P(), P(), P(), P()),
        out_specs=P("seq", "sp", None, None),
        check_vma=False,
    )
```

```python
import jax
import jax.numpy as jnp
from jax import lax
from jax.experimental import pallas as pl
from jax.experimental.pallas import tpu as pltpu
from jax.sharding import PartitionSpec as P

F32 = jnp.float32
BF16 = jnp.bfloat16
MESH = pl.DeviceIdType.MESH
TAPS = 3


def kernel(
    x_ref, gain_ref, cw_ref, cb_ref, tw_ref, tb_ref, clips_ref, out_ref,
    x_all, weight, time_w, gain_v, cb_v, tb_v, clips, joined, total, resid, before, latent,
    x_sem, w_sem, small_sem, send_sem, recv_sem, out_sem,
):
    frames, rows, cols, width = x_ref.shape
    lag = TAPS - 1
    deep = TAPS * width
    seq_count, sp_count = lax.axis_size("seq"), lax.axis_size("sp")
    seq, sp = lax.axis_index("seq"), lax.axis_index("sp")
    has_back, has_next = seq > 0, seq < seq_count - 1
    has_above, has_below = sp > 0, sp < sp_count - 1

    barrier = pltpu.get_barrier_semaphore()

    def greet(condition, device):
        @pl.when(condition)
        def _():
            pl.semaphore_signal(barrier, inc=1, device_id=device, device_id_type=MESH)

    greet(has_above, (seq, sp - 1))
    greet(has_below, (seq, sp + 1))
    greet(has_back, (seq - 1, sp))
    greet(has_back & has_above, (seq - 1, sp - 1))
    greet(has_back & has_below, (seq - 1, sp + 1))

    small = [
        pltpu.make_async_copy(source, target, small_sem.at[i])
        for i, (source, target) in enumerate((
                (gain_ref, gain_v), (cb_ref, cb_v), (tb_ref, tb_v), (clips_ref, clips)
            ))
    ]
    loads = [
        pltpu.make_async_copy(x_ref.at[t], x_all.at[lag + t, pl.ds(1, rows)], x_sem.at[t])
        for t in range(frames)
    ]

    def weight_load(slot, first, size):
        return [
            pltpu.make_async_copy(
                cw_ref.at[k, pl.ds(first, size)],
                weight.at[pl.ds(first, size), pl.ds(k * width, width)],
                w_sem.at[slot + k],
            )
            for k in range(TAPS)
        ]

    head, tail = weight_load(0, 0, deep), weight_load(TAPS, deep, 2 * deep)
    time_load = pltpu.make_async_copy(tw_ref, time_w, w_sem.at[2 * TAPS])
    small[0].start()
    for t in (3, 2, 1, 5, 4, 0):
        loads[t].start()
    for copy in head:
        copy.start()

    def count(condition):
        return jnp.where(condition, 1, 0)

    beside_me = count(has_above) + count(has_below)
    pl.semaphore_wait(barrier, beside_me + count(has_next) * (1 + beside_me))

    class Send:
        def __init__(self, slot, source, target, device, leaves, comes):
            self.copy = pltpu.make_async_remote_copy(
                src_ref=source, dst_ref=target,
                send_sem=send_sem.at[slot], recv_sem=recv_sem.at[slot],
                device_id=device, device_id_type=MESH,
            )
            self.leaves, self.comes = leaves, comes
            pl.when(leaves)(self.copy.start)

            @pl.when(jnp.logical_not(comes))
            def _():
                target[...] = jnp.zeros(target.shape, target.dtype)

        def wait_recv(self):
            pl.when(self.comes)(self.copy.wait_recv)

        def wait_send(self):
            pl.when(self.leaves)(self.copy.wait_send)

    last = pl.ds(frames - lag, lag)
    own, past = pl.ds(lag, frames), pl.ds(0, lag)
    up, down = (seq, sp - 1), (seq, sp + 1)
    above = Send(0, x_ref.at[:, rows - 1], x_all.at[own, 0], down, has_below, has_above)
    below = Send(1, x_ref.at[:, 0], x_all.at[own, rows + 1], up, has_above, has_below)
    earlier = [
        Send(
            2, x_ref.at[last], x_all.at[past, pl.ds(1, rows)], (seq + 1, sp), has_next, has_back
        ),
        Send(
            3, x_ref.at[last, rows - 1], x_all.at[past, 0], (seq + 1, sp + 1),
            has_next & has_below, has_back & has_above,
        ),
        Send(
            4, x_ref.at[last, 0], x_all.at[past, rows + 1], (seq + 1, sp - 1),
            has_next & has_above, has_back & has_below,
        ),
    ]

    small[0].wait()
    half_gain = gain_v[...].reshape(1, width) * 0.5
    column = lax.broadcasted_iota(jnp.int32, (cols, width), 0)

    def normalize(s, r, factor=None):
        values = x_all[s, r].astype(F32)
        scale = lax.rsqrt(jnp.mean(values * values, axis=-1, keepdims=True) + 1e-06)
        if factor is not None:
            scale = scale * factor
        half = values * scale * half_gain
        act = half + half * jnp.tanh(half)
        joined[s, r, :, pl.ds(width, width)] = act.astype(BF16)
        ahead = jnp.where(column == 0, 0.0, pltpu.roll(act, 1, 0))
        joined[s, r, :, pl.ds(0, width)] = ahead.astype(BF16)
        behind = jnp.where(column == cols - 1, 0.0, pltpu.roll(act, cols - 1, 0))
        joined[s, r, :, pl.ds(2 * width, width)] = behind.astype(BF16)

    queue = []

    def beside(count):
        for _ in range(min(count, len(queue))):
            normalize(*queue.pop(0))

    seen = set()
    inner, edge, whole = (1, rows - 1), None, (0, rows)

    def rows_of(s, part, d):
        if part is edge:
            pair = [joined[s, d], joined[s, rows - 1 + d]]
            return jnp.concatenate(pair, 0)
        lo, hi = part
        return joined[s, lo + d : hi + d].reshape((hi - lo) * cols, deep)

    def conv(sources, part, first=0, count=TAPS, final=()):
        left = jnp.concatenate(
            [
                jnp.concatenate([rows_of(s, part, d) for s in sources], 0)
                for d in range(first, first + count)
            ],
            1,
        )
        taps = [k for k in range(TAPS) if 0 <= sources[0] - k < frames]
        product = jnp.dot(
            left,
            weight[first * deep : (first + count) * deep, taps[0] * width : (taps[-1] + 1) * width],
            preferred_element_type=F32,
        )
        size = left.shape[0] // len(sources)
        sums = {}
        for i, s in enumerate(sources):
            for n, k in enumerate(taps):
                piece = product[i * size : (i + 1) * size, n * width : (n + 1) * width]
                sums[s - k] = sums[s - k] + piece if s - k in sums else piece
        for t, piece in sums.items():
            spots = [0, rows - 1] if part is edge else [slice(*part)]
            for i, spot in enumerate(spots):
                share = piece.shape[0] // len(spots)
                value = piece[i * share : (i + 1) * share]
                value = value.reshape(((share // cols,) if part is not edge else ()) + (cols, width))
                marks = [(t, r) for r in (range(*part) if part is not edge else [spot])]
                if marks[0] in seen:
                    value = total[t, spot] + value
                seen.update(marks)
                if t in final:
                    finish(t, value)
                else:
                    total[t, spot] = value

    def finish(t, summed):
        values = x_all[lag + t, 1 : rows + 1].astype(F32)
        done = values + summed + cb_v[...].reshape(1, 1, width)
        resid[t + 1] = done.reshape(rows * cols, width).astype(BF16)

    def project(j):
        left = jnp.concatenate([resid[2 * j + k] for k in range(TAPS)], 1)
        done = jnp.dot(left, time_w[...], preferred_element_type=F32) + tb_v[...].reshape(1, width)
        latent[j] = done.reshape(rows, cols, width).astype(BF16)
        copy = pltpu.make_async_copy(latent.at[j], out_ref.at[j], out_sem.at[j])
        copy.start()
        return copy

    for t in (3, 2, 1):
        loads[t].wait()
    for copy in tail + [time_load] + small[1:]:
        copy.start()
    for t in (3, 2, 1):
        for r in range(1, rows + 1):
            normalize(lag + t, r)
    for t in (5, 4, 0):
        loads[t].wait()
        queue.extend((lag + t, r) for r in range(1, rows + 1))
    for copy in head:
        copy.wait()
    for s in (5, 4, 3):
        conv((s,), inner, 0, 1)
        beside(4)
    for copy in tail + small[1:]:
        copy.wait()
    for s in (5, 4):
        conv((s,), inner, 1, 2)
        beside(6)
    above.wait_recv()
    below.wait_recv()
    for s in (5, 4, 3):
        normalize(s, 0)
        normalize(s, rows + 1)
    for s in (7, 6, 2):
        queue.extend(((s, 0), (s, rows + 1)))
    conv((3,), inner, 1, 2)
    conv((5, 4, 3), edge)
    beside(len(queue))
    finish(3, total[3])
    conv((7,), whole)
    conv((6,), whole, final=(5, 4))
    before_copy = Send(5, resid.at[frames], before, (seq + 1, sp), has_next, has_back)
    time_load.wait()
    outs = [project(2)]
    for copy in earlier:
        copy.wait_recv()
    opening = jnp.int32(0)
    start = jnp.int32(0)
    for j in range(clips.shape[0]):
        opening = opening + jnp.where(start == seq, 1, 0)
        start = start + clips[j]
    keep = (1 - opening).astype(F32)
    for s in reversed(range(lag)):
        for r in range(rows + 2):
            normalize(s, r, keep)
    conv((2,), whole, final=(2,))
    conv((1,), whole, final=(1,))
    outs.append(project(1))
    conv((0,), whole, final=(0,))
    before_copy.wait_recv()
    resid[0] = (before[...].astype(F32) * keep).astype(BF16)
    outs.append(project(0))
    for copy in [above, below, *earlier, before_copy]:
        copy.wait_send()
    for copy in outs:
        copy.wait()


def per_device(frames_in, gain, conv_weight, conv_bias, time_weight, time_bias, clip_lengths):
    frames, rows, cols, width = frames_in.shape
    deep = TAPS * TAPS * width
    lag = TAPS - 1
    anywhere = pl.BlockSpec(memory_space=pl.ANY)
    flops = 2 * frames * rows * cols * width * (TAPS * deep + TAPS * width // 2)
    return pl.pallas_call(
        kernel,
        out_shape=jax.ShapeDtypeStruct((frames // 2, rows, cols, width), BF16),
        in_specs=[anywhere] * 7,
        out_specs=anywhere,
        scratch_shapes=[
            pltpu.VMEM((frames + lag, rows + 2, cols, width), BF16),
            pltpu.VMEM((deep, TAPS * width), BF16),
            pltpu.VMEM((TAPS * width, width), BF16),
            pltpu.VMEM((width,), F32),
            pltpu.VMEM((width,), F32),
            pltpu.VMEM((width,), F32),
            pltpu.SMEM(clip_lengths.shape, jnp.int32),
            pltpu.VMEM((frames + lag, rows + 2, cols, TAPS * width), BF16),
            pltpu.VMEM((frames, rows, cols, width), F32),
            pltpu.VMEM((frames + 1, rows * cols, width), BF16),
            pltpu.VMEM((rows * cols, width), BF16),
            pltpu.VMEM((frames // 2, rows, cols, width), BF16),
            pltpu.SemaphoreType.DMA((frames,)),
            pltpu.SemaphoreType.DMA((2 * TAPS + 1,)),
            pltpu.SemaphoreType.DMA((4,)),
            pltpu.SemaphoreType.DMA((6,)),
            pltpu.SemaphoreType.DMA((6,)),
            pltpu.SemaphoreType.DMA((frames // 2,)),
        ],
        compiler_params=pltpu.CompilerParams(
            collective_id=0, has_side_effects=True, vmem_limit_bytes=56 * 2**20
        ),
        cost_estimate=pl.CostEstimate(flops=flops, bytes_accessed=12_000_000, transcendentals=0),
        name="residual_block",
    )(
        frames_in,
        gain,
        conv_weight.reshape(TAPS, deep, width),
        conv_bias,
        time_weight.reshape(TAPS * width, width),
        time_bias,
        clip_lengths,
    )


def solution(mesh):
    return jax.shard_map(
        per_device,
        mesh=mesh,
        in_specs=(P("seq", "sp", None, None), P(), P(), P(), P(), P(), P()),
        out_specs=P("seq", "sp", None, None),
        check_vma=False,
    )
```

```python
import jax
import jax.numpy as jnp
from jax import lax
from jax.experimental import pallas as pl
from jax.experimental.pallas import tpu as pltpu
from jax.sharding import PartitionSpec as P

F32 = jnp.float32
BF16 = jnp.bfloat16
MESH = pl.DeviceIdType.MESH
TAPS = 3
PIECE = 256


def kernel(
    x_ref, gain_ref, cw_ref, cb_ref, tw_ref, tb_ref, clips_ref, out_ref,
    x_all, weight, time_w, gain_v, cb_v, tb_v, clips, joined, total, resid, before, latent,
    x_sem, w_sem, small_sem, send_sem, recv_sem, out_sem,
):
    frames, rows, cols, width = x_ref.shape
    lag = TAPS - 1
    deep = TAPS * width
    seq_count, sp_count = lax.axis_size("seq"), lax.axis_size("sp")
    seq, sp = lax.axis_index("seq"), lax.axis_index("sp")
    has_back, has_next = seq > 0, seq < seq_count - 1
    has_above, has_below = sp > 0, sp < sp_count - 1

    barrier = pltpu.get_barrier_semaphore()

    def greet(condition, device):
        @pl.when(condition)
        def _():
            pl.semaphore_signal(barrier, inc=1, device_id=device, device_id_type=MESH)

    greet(has_above, (seq, sp - 1))
    greet(has_below, (seq, sp + 1))
    greet(has_back, (seq - 1, sp))
    greet(has_back & has_above, (seq - 1, sp - 1))
    greet(has_back & has_below, (seq - 1, sp + 1))

    small = [
        pltpu.make_async_copy(source, target, small_sem.at[i])
        for i, (source, target) in enumerate((
                (gain_ref, gain_v), (cb_ref, cb_v), (tb_ref, tb_v), (clips_ref, clips)
            ))
    ]
    loads = [
        pltpu.make_async_copy(x_ref.at[t], x_all.at[lag + t, pl.ds(1, rows)], x_sem.at[t])
        for t in range(frames)
    ]

    def weight_load(slot, first, size):
        return [
            pltpu.make_async_copy(
                cw_ref.at[k, pl.ds(first, size)],
                weight.at[pl.ds(first, size), pl.ds(k * width, width)],
                w_sem.at[slot + k],
            )
            for k in range(TAPS)
        ]

    head, tail = weight_load(0, 0, deep), weight_load(TAPS, deep, 2 * deep)
    time_load = pltpu.make_async_copy(tw_ref, time_w, w_sem.at[2 * TAPS])
    small[0].start()
    for t in (3, 2, 1, 5, 4, 0):
        loads[t].start()
    for copy in head:
        copy.start()

    small[0].wait()
    half_gain = gain_v[...].reshape(1, width) * 0.5
    column = lax.broadcasted_iota(jnp.int32, (cols, width), 0)

    def normalize(s, r, factor=None):
        values = x_all[s, r].astype(F32)
        scale = lax.rsqrt(jnp.mean(values * values, axis=-1, keepdims=True) + 1e-06)
        if factor is not None:
            scale = scale * factor
        half = values * scale * half_gain
        act = half + half * jnp.tanh(half)
        joined[s, r, :, pl.ds(width, width)] = act.astype(BF16)
        ahead = jnp.where(column == 0, 0.0, pltpu.roll(act, 1, 0))
        joined[s, r, :, pl.ds(0, width)] = ahead.astype(BF16)
        behind = jnp.where(column == cols - 1, 0.0, pltpu.roll(act, cols - 1, 0))
        joined[s, r, :, pl.ds(2 * width, width)] = behind.astype(BF16)

    queue = []

    def beside(count):
        for _ in range(min(count, len(queue))):
            normalize(*queue.pop(0))

    seen = set()
    inner, edge, whole = (1, rows - 1), None, (0, rows)

    def rows_of(s, part, d):
        if part is edge:
            pair = [joined[s, d], joined[s, rows - 1 + d]]
            return jnp.concatenate(pair, 0)
        lo, hi = part
        return joined[s, lo + d : hi + d].reshape((hi - lo) * cols, deep)

    def conv(sources, part, first=0, count=TAPS, final=(), rate=0):
        left = jnp.concatenate(
            [
                jnp.concatenate([rows_of(s, part, d) for s in sources], 0)
                for d in range(first, first + count)
            ],
            1,
        )
        taps = [k for k in range(TAPS) if 0 <= sources[0] - k < frames]
        deepest, stop = slice(first * deep, (first + count) * deep), (taps[-1] + 1) * width
        pieces = []
        for column in range(taps[0] * width, stop, PIECE):
            columns = slice(column, min(column + PIECE, stop))
            pieces.append(jnp.dot(left, weight[deepest, columns], preferred_element_type=F32))
            beside(rate)
        product = jnp.concatenate(pieces, 1)
        size = left.shape[0] // len(sources)
        sums = {}
        for i, s in enumerate(sources):
            for n, k in enumerate(taps):
                piece = product[i * size : (i + 1) * size, n * width : (n + 1) * width]
                sums[s - k] = sums[s - k] + piece if s - k in sums else piece
        for t, piece in sums.items():
            spots = [0, rows - 1] if part is edge else [slice(*part)]
            for i, spot in enumerate(spots):
                share = piece.shape[0] // len(spots)
                value = piece[i * share : (i + 1) * share]
                value = value.reshape(((share // cols,) if part is not edge else ()) + (cols, width))
                marks = [(t, r) for r in (range(*part) if part is not edge else [spot])]
                if marks[0] in seen:
                    value = total[t, spot] + value
                seen.update(marks)
                if t in final:
                    finish(t, value)
                else:
                    total[t, spot] = value

    def finish(t, summed):
        values = x_all[lag + t, 1 : rows + 1].astype(F32)
        done = values + summed + cb_v[...].reshape(1, 1, width)
        resid[t + 1] = done.reshape(rows * cols, width).astype(BF16)

    def project(j):
        left = jnp.concatenate([resid[2 * j + k] for k in range(TAPS)], 1)
        done = jnp.dot(left, time_w[...], preferred_element_type=F32) + tb_v[...].reshape(1, width)
        latent[j] = done.reshape(rows, cols, width).astype(BF16)
        copy = pltpu.make_async_copy(latent.at[j], out_ref.at[j], out_sem.at[j])
        copy.start()
        return copy

    for t in (3, 2, 1):
        loads[t].wait()
    for copy in tail + [time_load] + small[1:]:
        copy.start()
    for t in (3, 2, 1):
        for r in range(1, rows + 1):
            normalize(lag + t, r)
    def count(condition):
        return jnp.where(condition, 1, 0)

    beside_me = count(has_above) + count(has_below)
    pl.semaphore_wait(barrier, beside_me + count(has_next) * (1 + beside_me))

    class Send:
        def __init__(self, slot, source, target, device, leaves, comes):
            self.copy = pltpu.make_async_remote_copy(
                src_ref=source, dst_ref=target,
                send_sem=send_sem.at[slot], recv_sem=recv_sem.at[slot],
                device_id=device, device_id_type=MESH,
            )
            self.leaves, self.comes = leaves, comes
            pl.when(leaves)(self.copy.start)

            @pl.when(jnp.logical_not(comes))
            def _():
                target[...] = jnp.zeros(target.shape, target.dtype)

        def wait_recv(self):
            pl.when(self.comes)(self.copy.wait_recv)

        def wait_send(self):
            pl.when(self.leaves)(self.copy.wait_send)

    last = pl.ds(frames - lag, lag)
    past = pl.ds(0, lag)
    up, down = (seq, sp - 1), (seq, sp + 1)

    def edges(slot, first, size):
        here, there = pl.ds(first, size), pl.ds(lag + first, size)
        return [
            Send(
                slot, x_ref.at[here, rows - 1], x_all.at[there, 0], down, has_below, has_above
            ),
            Send(
                slot + 1, x_ref.at[here, 0], x_all.at[there, rows + 1], up, has_above, has_below
            ),
        ]

    middle = edges(6, 1, 3)
    outer = edges(0, 4, 2) + edges(8, 0, 1)
    earlier = [
        Send(
            2, x_ref.at[last], x_all.at[past, pl.ds(1, rows)], (seq + 1, sp), has_next, has_back
        ),
        Send(
            3, x_ref.at[last, rows - 1], x_all.at[past, 0], (seq + 1, sp + 1),
            has_next & has_below, has_back & has_above,
        ),
        Send(
            4, x_ref.at[last, 0], x_all.at[past, rows + 1], (seq + 1, sp - 1),
            has_next & has_above, has_back & has_below,
        ),
    ]

    for t in (5, 4, 0):
        loads[t].wait()
        queue.extend((lag + t, r) for r in range(1, rows + 1))
    for copy in head:
        copy.wait()
    for s in (5, 4, 3):
        conv((s,), inner, 0, 1, rate=1)
    for copy in tail + small[1:]:
        copy.wait()
    for s in (5, 4):
        conv((s,), inner, 1, 2, rate=1)
    for copy in middle:
        copy.wait_recv()
    queue[:0] = [(s, r) for s in (5, 4, 3) for r in (0, rows + 1)]
    conv((3,), inner, 1, 2, rate=2)
    for copy in outer:
        copy.wait_recv()
    queue[:0] = [(s, r) for s in (7, 6) for r in (0, rows + 1)]
    queue.extend((2, r) for r in (0, rows + 1))
    conv((5, 4, 3), edge, rate=2)
    finish(3, total[3])
    beside(len([item for item in queue if item[0] > 2]))
    conv((7,), whole)
    conv((6,), whole, final=(5, 4))
    before_copy = Send(5, resid.at[frames], before, (seq + 1, sp), has_next, has_back)
    time_load.wait()
    outs = [project(2)]
    for copy in earlier:
        copy.wait_recv()
    opening = jnp.int32(0)
    start = jnp.int32(0)
    for j in range(clips.shape[0]):
        opening = opening + jnp.where(start == seq, 1, 0)
        start = start + clips[j]
    keep = (1 - opening).astype(F32)
    beside(len(queue))
    queue.extend((s, r, keep) for s in reversed(range(lag)) for r in range(rows + 2))
    conv((2,), whole, final=(2,), rate=4)
    conv((1,), whole, final=(1,))
    outs.append(project(1))
    conv((0,), whole, final=(0,))
    before_copy.wait_recv()
    resid[0] = (before[...].astype(F32) * keep).astype(BF16)
    outs.append(project(0))
    for copy in [*middle, *outer, *earlier, before_copy]:
        copy.wait_send()
    for copy in outs:
        copy.wait()


def per_device(frames_in, gain, conv_weight, conv_bias, time_weight, time_bias, clip_lengths):
    frames, rows, cols, width = frames_in.shape
    deep = TAPS * TAPS * width
    lag = TAPS - 1
    anywhere = pl.BlockSpec(memory_space=pl.ANY)
    flops = 2 * frames * rows * cols * width * (TAPS * deep + TAPS * width // 2)
    return pl.pallas_call(
        kernel,
        out_shape=jax.ShapeDtypeStruct((frames // 2, rows, cols, width), BF16),
        in_specs=[anywhere] * 7,
        out_specs=anywhere,
        scratch_shapes=[
            pltpu.VMEM((frames + lag, rows + 2, cols, width), BF16),
            pltpu.VMEM((deep, TAPS * width), BF16),
            pltpu.VMEM((TAPS * width, width), BF16),
            pltpu.VMEM((width,), F32),
            pltpu.VMEM((width,), F32),
            pltpu.VMEM((width,), F32),
            pltpu.SMEM(clip_lengths.shape, jnp.int32),
            pltpu.VMEM((frames + lag, rows + 2, cols, TAPS * width), BF16),
            pltpu.VMEM((frames, rows, cols, width), F32),
            pltpu.VMEM((frames + 1, rows * cols, width), BF16),
            pltpu.VMEM((rows * cols, width), BF16),
            pltpu.VMEM((frames // 2, rows, cols, width), BF16),
            pltpu.SemaphoreType.DMA((frames,)),
            pltpu.SemaphoreType.DMA((2 * TAPS + 1,)),
            pltpu.SemaphoreType.DMA((4,)),
            pltpu.SemaphoreType.DMA((10,)),
            pltpu.SemaphoreType.DMA((10,)),
            pltpu.SemaphoreType.DMA((frames // 2,)),
        ],
        compiler_params=pltpu.CompilerParams(
            collective_id=0, has_side_effects=True, vmem_limit_bytes=56 * 2**20
        ),
        cost_estimate=pl.CostEstimate(flops=flops, bytes_accessed=12_000_000, transcendentals=0),
        name="residual_block",
    )(
        frames_in,
        gain,
        conv_weight.reshape(TAPS, deep, width),
        conv_bias,
        time_weight.reshape(TAPS * width, width),
        time_bias,
        clip_lengths,
    )


def solution(mesh):
    return jax.shard_map(
        per_device,
        mesh=mesh,
        in_specs=(P("seq", "sp", None, None), P(), P(), P(), P(), P(), P()),
        out_specs=P("seq", "sp", None, None),
        check_vma=False,
    )
```

```python
import jax
import jax.numpy as jnp
from jax import lax
from jax.experimental import pallas as pl
from jax.experimental.pallas import tpu as pltpu
from jax.sharding import PartitionSpec as P

F32 = jnp.float32
BF16 = jnp.bfloat16
MESH = pl.DeviceIdType.MESH
TAPS = 3
PIECE = 256


def kernel(
    x_ref, gain_ref, cw_ref, cb_ref, tw_ref, tb_ref, clips_ref, out_ref,
    x_all, weight, time_w, gain_v, cb_v, tb_v, clips, joined, total, resid, before, latent,
    x_sem, w_sem, small_sem, send_sem, recv_sem, out_sem,
):
    frames, rows, cols, width = x_ref.shape
    lag = TAPS - 1
    deep = TAPS * width
    seq_count, sp_count = lax.axis_size("seq"), lax.axis_size("sp")
    seq, sp = lax.axis_index("seq"), lax.axis_index("sp")
    has_back, has_next = seq > 0, seq < seq_count - 1
    has_above, has_below = sp > 0, sp < sp_count - 1

    barrier = pltpu.get_barrier_semaphore()

    def greet(condition, device):
        @pl.when(condition)
        def _():
            pl.semaphore_signal(barrier, inc=1, device_id=device, device_id_type=MESH)

    greet(has_above, (seq, sp - 1))
    greet(has_below, (seq, sp + 1))
    greet(has_back, (seq - 1, sp))
    greet(has_back & has_above, (seq - 1, sp - 1))
    greet(has_back & has_below, (seq - 1, sp + 1))

    small = [
        pltpu.make_async_copy(source, target, small_sem.at[i])
        for i, (source, target) in enumerate((
                (gain_ref, gain_v), (cb_ref, cb_v), (tb_ref, tb_v), (clips_ref, clips)
            ))
    ]
    loads = [
        pltpu.make_async_copy(x_ref.at[t], x_all.at[lag + t, pl.ds(1, rows)], x_sem.at[t])
        for t in range(frames)
    ]

    def weight_load(slot, first, size):
        return [
            pltpu.make_async_copy(
                cw_ref.at[k, pl.ds(first, size)],
                weight.at[pl.ds(first, size), pl.ds(k * width, width)],
                w_sem.at[slot + k],
            )
            for k in range(TAPS)
        ]

    head, tail = weight_load(0, 0, deep), weight_load(TAPS, deep, 2 * deep)
    time_load = pltpu.make_async_copy(tw_ref, time_w, w_sem.at[2 * TAPS])
    small[0].start()
    for t in (3, 2, 1, 5, 4, 0):
        loads[t].start()
    for copy in head:
        copy.start()

    small[0].wait()
    half_gain = gain_v[...].reshape(1, width) * 0.5
    column = lax.broadcasted_iota(jnp.int32, (cols, width), 0)

    def normalize(s, r, factor=None):
        values = x_all[s, r].astype(F32)
        scale = lax.rsqrt(jnp.mean(values * values, axis=-1, keepdims=True) + 1e-06)
        if factor is not None:
            scale = scale * factor
        half = values * scale * half_gain
        act = half + half * jnp.tanh(half)
        joined[s, r, :, pl.ds(width, width)] = act.astype(BF16)
        ahead = jnp.where(column == 0, 0.0, pltpu.roll(act, 1, 0))
        joined[s, r, :, pl.ds(0, width)] = ahead.astype(BF16)
        behind = jnp.where(column == cols - 1, 0.0, pltpu.roll(act, cols - 1, 0))
        joined[s, r, :, pl.ds(2 * width, width)] = behind.astype(BF16)

    queue = []

    def beside(count):
        for _ in range(min(count, len(queue))):
            normalize(*queue.pop(0))

    seen = set()
    inner, edge, whole = (1, rows - 1), None, (0, rows)

    def rows_of(s, part, d):
        if part is edge:
            pair = [joined[s, d], joined[s, rows - 1 + d]]
            return jnp.concatenate(pair, 0)
        lo, hi = part
        return joined[s, lo + d : hi + d].reshape((hi - lo) * cols, deep)

    def conv(sources, part, first=0, count=TAPS, final=(), rate=0):
        left = jnp.concatenate(
            [
                jnp.concatenate([rows_of(s, part, d) for s in sources], 0)
                for d in range(first, first + count)
            ],
            1,
        )
        taps = [k for k in range(TAPS) if 0 <= sources[0] - k < frames]
        deepest, stop = slice(first * deep, (first + count) * deep), (taps[-1] + 1) * width
        pieces = []
        for column in range(taps[0] * width, stop, PIECE):
            columns = slice(column, min(column + PIECE, stop))
            pieces.append(jnp.dot(left, weight[deepest, columns], preferred_element_type=F32))
            beside(rate)
        product = jnp.concatenate(pieces, 1)
        size = left.shape[0] // len(sources)
        sums = {}
        for i, s in enumerate(sources):
            for n, k in enumerate(taps):
                piece = product[i * size : (i + 1) * size, n * width : (n + 1) * width]
                sums[s - k] = sums[s - k] + piece if s - k in sums else piece
        for t, piece in sums.items():
            spots = [0, rows - 1] if part is edge else [slice(*part)]
            for i, spot in enumerate(spots):
                share = piece.shape[0] // len(spots)
                value = piece[i * share : (i + 1) * share]
                value = value.reshape(((share // cols,) if part is not edge else ()) + (cols, width))
                marks = [(t, r) for r in (range(*part) if part is not edge else [spot])]
                if marks[0] in seen:
                    value = total[t, spot] + value
                seen.update(marks)
                if t in final:
                    finish(t, value)
                else:
                    total[t, spot] = value

    def finish(t, summed):
        values = x_all[lag + t, 1 : rows + 1].astype(F32)
        done = values + summed + cb_v[...].reshape(1, 1, width)
        resid[t + 1] = done.reshape(rows * cols, width).astype(BF16)

    def project(j):
        left = jnp.concatenate([resid[2 * j + k] for k in range(TAPS)], 1)
        done = jnp.dot(left, time_w[...], preferred_element_type=F32) + tb_v[...].reshape(1, width)
        latent[j] = done.reshape(rows, cols, width).astype(BF16)
        copy = pltpu.make_async_copy(latent.at[j], out_ref.at[j], out_sem.at[j])
        copy.start()
        return copy

    for t in (3, 2, 1):
        loads[t].wait()
    for copy in tail + [time_load] + small[1:]:
        copy.start()
    for t in (3, 2, 1):
        for r in range(1, rows + 1):
            normalize(lag + t, r)
    for t in (5, 4, 0):
        loads[t].wait()
        queue.extend((lag + t, r) for r in range(1, rows + 1))
    for copy in head:
        copy.wait()
    for s in (5, 4, 3):
        conv((s,), inner, 0, 1, rate=1)

    def count(condition):
        return jnp.where(condition, 1, 0)

    beside_me = count(has_above) + count(has_below)
    pl.semaphore_wait(barrier, beside_me + count(has_next) * (1 + beside_me))

    class Send:
        def __init__(self, slot, source, target, device, leaves, comes):
            self.copy = pltpu.make_async_remote_copy(
                src_ref=source, dst_ref=target,
                send_sem=send_sem.at[slot], recv_sem=recv_sem.at[slot],
                device_id=device, device_id_type=MESH,
            )
            self.leaves, self.comes = leaves, comes
            pl.when(leaves)(self.copy.start)

            @pl.when(jnp.logical_not(comes))
            def _():
                target[...] = jnp.zeros(target.shape, target.dtype)

        def wait_recv(self):
            pl.when(self.comes)(self.copy.wait_recv)

        def wait_send(self):
            pl.when(self.leaves)(self.copy.wait_send)

    last = pl.ds(frames - lag, lag)
    past = pl.ds(0, lag)
    up, down = (seq, sp - 1), (seq, sp + 1)

    def edges(slot, first, size):
        here, there = pl.ds(first, size), pl.ds(lag + first, size)
        return [
            Send(
                slot, x_ref.at[here, rows - 1], x_all.at[there, 0], down, has_below, has_above
            ),
            Send(
                slot + 1, x_ref.at[here, 0], x_all.at[there, rows + 1], up, has_above, has_below
            ),
        ]

    middle = edges(6, 1, 3)
    outer = edges(0, 4, 2) + edges(8, 0, 1)
    earlier = [
        Send(
            2, x_ref.at[last], x_all.at[past, pl.ds(1, rows)], (seq + 1, sp), has_next, has_back
        ),
        Send(
            3, x_ref.at[last, rows - 1], x_all.at[past, 0], (seq + 1, sp + 1),
            has_next & has_below, has_back & has_above,
        ),
        Send(
            4, x_ref.at[last, 0], x_all.at[past, rows + 1], (seq + 1, sp - 1),
            has_next & has_above, has_back & has_below,
        ),
    ]

    for copy in tail + small[1:]:
        copy.wait()
    for s in (5, 4, 3):
        conv((s,), inner, 1, 2, rate=1)
    for copy in middle + outer:
        copy.wait_recv()
    for s in (5, 4, 3):
        normalize(s, 0)
        normalize(s, rows + 1)
    queue[:0] = [(s, r) for s in (7, 6) for r in (0, rows + 1)]
    queue.extend((2, r) for r in (0, rows + 1))
    conv((5, 4, 3), edge, rate=2)
    finish(3, total[3])
    beside(len([item for item in queue if item[0] > 2]))
    conv((7,), whole)
    conv((6,), whole, final=(5, 4))
    before_copy = Send(5, resid.at[frames], before, (seq + 1, sp), has_next, has_back)
    time_load.wait()
    outs = [project(2)]
    for copy in earlier:
        copy.wait_recv()
    opening = jnp.int32(0)
    start = jnp.int32(0)
    for j in range(clips.shape[0]):
        opening = opening + jnp.where(start == seq, 1, 0)
        start = start + clips[j]
    keep = (1 - opening).astype(F32)
    beside(len(queue))
    queue.extend((s, r, keep) for s in reversed(range(lag)) for r in range(rows + 2))
    conv((2,), whole, final=(2,), rate=4)
    conv((1,), whole, final=(1,))
    outs.append(project(1))
    conv((0,), whole, final=(0,))
    before_copy.wait_recv()
    resid[0] = (before[...].astype(F32) * keep).astype(BF16)
    outs.append(project(0))
    for copy in [*middle, *outer, *earlier, before_copy]:
        copy.wait_send()
    for copy in outs:
        copy.wait()


def per_device(frames_in, gain, conv_weight, conv_bias, time_weight, time_bias, clip_lengths):
    frames, rows, cols, width = frames_in.shape
    deep = TAPS * TAPS * width
    lag = TAPS - 1
    anywhere = pl.BlockSpec(memory_space=pl.ANY)
    flops = 2 * frames * rows * cols * width * (TAPS * deep + TAPS * width // 2)
    return pl.pallas_call(
        kernel,
        out_shape=jax.ShapeDtypeStruct((frames // 2, rows, cols, width), BF16),
        in_specs=[anywhere] * 7,
        out_specs=anywhere,
        scratch_shapes=[
            pltpu.VMEM((frames + lag, rows + 2, cols, width), BF16),
            pltpu.VMEM((deep, TAPS * width), BF16),
            pltpu.VMEM((TAPS * width, width), BF16),
            pltpu.VMEM((width,), F32),
            pltpu.VMEM((width,), F32),
            pltpu.VMEM((width,), F32),
            pltpu.SMEM(clip_lengths.shape, jnp.int32),
            pltpu.VMEM((frames + lag, rows + 2, cols, TAPS * width), BF16),
            pltpu.VMEM((frames, rows, cols, width), F32),
            pltpu.VMEM((frames + 1, rows * cols, width), BF16),
            pltpu.VMEM((rows * cols, width), BF16),
            pltpu.VMEM((frames // 2, rows, cols, width), BF16),
            pltpu.SemaphoreType.DMA((frames,)),
            pltpu.SemaphoreType.DMA((2 * TAPS + 1,)),
            pltpu.SemaphoreType.DMA((4,)),
            pltpu.SemaphoreType.DMA((10,)),
            pltpu.SemaphoreType.DMA((10,)),
            pltpu.SemaphoreType.DMA((frames // 2,)),
        ],
        compiler_params=pltpu.CompilerParams(
            collective_id=0, has_side_effects=True, vmem_limit_bytes=56 * 2**20
        ),
        cost_estimate=pl.CostEstimate(flops=flops, bytes_accessed=12_000_000, transcendentals=0),
        name="residual_block",
    )(
        frames_in,
        gain,
        conv_weight.reshape(TAPS, deep, width),
        conv_bias,
        time_weight.reshape(TAPS * width, width),
        time_bias,
        clip_lengths,
    )


def solution(mesh):
    return jax.shard_map(
        per_device,
        mesh=mesh,
        in_specs=(P("seq", "sp", None, None), P(), P(), P(), P(), P(), P()),
        out_specs=P("seq", "sp", None, None),
        check_vma=False,
    )
```

```python
import jax
import jax.numpy as jnp
from jax import lax
from jax.experimental import pallas as pl
from jax.experimental.pallas import tpu as pltpu
from jax.sharding import PartitionSpec as P

F32 = jnp.float32
BF16 = jnp.bfloat16
MESH = pl.DeviceIdType.MESH
TAPS = 3
PIECE = 256


def kernel(
    x_ref, gain_ref, cw_ref, cb_ref, tw_ref, tb_ref, clips_ref, out_ref,
    x_all, weight, time_w, gain_v, cb_v, tb_v, clips, joined, total, resid, before, latent,
    x_sem, w_sem, small_sem, send_sem, recv_sem, out_sem, ready_sem,
):
    frames, rows, cols, width = x_ref.shape
    lag = TAPS - 1
    deep = TAPS * width
    seq_count, sp_count = lax.axis_size("seq"), lax.axis_size("sp")
    seq, sp = lax.axis_index("seq"), lax.axis_index("sp")
    has_back, has_next = seq > 0, seq < seq_count - 1
    has_above, has_below = sp > 0, sp < sp_count - 1

    barrier = pltpu.get_barrier_semaphore()

    def greet(condition, device, semaphore=barrier):
        @pl.when(condition)
        def _():
            pl.semaphore_signal(semaphore, inc=1, device_id=device, device_id_type=MESH)

    greet(has_above, (seq, sp - 1))
    greet(has_below, (seq, sp + 1))
    greet(has_next, (seq + 1, sp))
    greet(has_next & has_above, (seq + 1, sp - 1))
    greet(has_next & has_below, (seq + 1, sp + 1))

    small = [
        pltpu.make_async_copy(source, target, small_sem.at[i])
        for i, (source, target) in enumerate((
                (gain_ref, gain_v), (cb_ref, cb_v), (tb_ref, tb_v), (clips_ref, clips)
            ))
    ]
    loads = [
        pltpu.make_async_copy(x_ref.at[t], x_all.at[lag + t, pl.ds(1, rows)], x_sem.at[t])
        for t in range(frames)
    ]

    def weight_load(slot, first, size):
        return [
            pltpu.make_async_copy(
                cw_ref.at[k, pl.ds(first, size)],
                weight.at[pl.ds(first, size), pl.ds(k * width, width)],
                w_sem.at[slot + k],
            )
            for k in range(TAPS)
        ]

    head, tail = weight_load(0, 0, deep), weight_load(TAPS, deep, 2 * deep)
    time_load = pltpu.make_async_copy(tw_ref, time_w, w_sem.at[2 * TAPS])
    small[0].start()
    for t in (3, 2, 1):
        loads[t].start()
    head[2].start()
    for t in (5, 4, 0):
        loads[t].start()

    small[0].wait()
    half_gain = gain_v[...].reshape(1, width) * 0.5
    column = lax.broadcasted_iota(jnp.int32, (cols, width), 0)

    def normalize(s, r, factor=None):
        values = x_all[s, r].astype(F32)
        scale = lax.rsqrt(jnp.mean(values * values, axis=-1, keepdims=True) + 1e-06)
        if factor is not None:
            scale = scale * factor
        half = values * scale * half_gain
        act = half + half * jnp.tanh(half)
        joined[s, r, :, pl.ds(width, width)] = act.astype(BF16)
        ahead = jnp.where(column == 0, 0.0, pltpu.roll(act, 1, 0))
        joined[s, r, :, pl.ds(0, width)] = ahead.astype(BF16)
        behind = jnp.where(column == cols - 1, 0.0, pltpu.roll(act, cols - 1, 0))
        joined[s, r, :, pl.ds(2 * width, width)] = behind.astype(BF16)

    queue = []

    def beside(count):
        for _ in range(min(count, len(queue))):
            normalize(*queue.pop(0))

    seen = set()
    inner, edge, whole = (1, rows - 1), None, (0, rows)

    def rows_of(s, part, d):
        if part is edge:
            pair = [joined[s, d], joined[s, rows - 1 + d]]
            return jnp.concatenate(pair, 0)
        lo, hi = part
        return joined[s, lo + d : hi + d].reshape((hi - lo) * cols, deep)

    def conv(sources, part, first=0, count=TAPS, final=(), rate=0, only=range(TAPS), midway=lambda: None):
        left = jnp.concatenate(
            [
                jnp.concatenate([rows_of(s, part, d) for s in sources], 0)
                for d in range(first, first + count)
            ],
            1,
        )
        taps = [k for k in only if 0 <= sources[0] - k < frames]
        deepest, stop = slice(first * deep, (first + count) * deep), (taps[-1] + 1) * width
        pieces = []
        for column in range(taps[0] * width, stop, PIECE):
            columns = slice(column, min(column + PIECE, stop))
            pieces.append(jnp.dot(left, weight[deepest, columns], preferred_element_type=F32))
            if column == taps[0] * width + 2 * PIECE:
                midway()
            beside(rate)
        product = jnp.concatenate(pieces, 1)
        size = left.shape[0] // len(sources)
        sums = {}
        for i, s in enumerate(sources):
            for n, k in enumerate(taps):
                piece = product[i * size : (i + 1) * size, n * width : (n + 1) * width]
                sums[s - k] = sums[s - k] + piece if s - k in sums else piece
        for t, piece in sums.items():
            spots = [0, rows - 1] if part is edge else [slice(*part)]
            for i, spot in enumerate(spots):
                share = piece.shape[0] // len(spots)
                value = piece[i * share : (i + 1) * share]
                value = value.reshape(((share // cols,) if part is not edge else ()) + (cols, width))
                marks = [(t, r) for r in (range(*part) if part is not edge else [spot])]
                if marks[0] in seen:
                    value = total[t, spot] + value
                seen.update(marks)
                if t in final:
                    finish(t, value)
                else:
                    total[t, spot] = value

    def finish(t, summed):
        values = x_all[lag + t, 1 : rows + 1].astype(F32)
        done = values + summed + cb_v[...].reshape(1, 1, width)
        resid[t + 1] = done.reshape(rows * cols, width).astype(BF16)

    def project(j):
        left = jnp.concatenate([resid[2 * j + k] for k in range(TAPS)], 1)
        done = jnp.dot(left, time_w[...], preferred_element_type=F32) + tb_v[...].reshape(1, width)
        latent[j] = done.reshape(rows, cols, width).astype(BF16)
        copy = pltpu.make_async_copy(latent.at[j], out_ref.at[j], out_sem.at[j])
        copy.start()
        return copy

    for t in (3, 2, 1):
        loads[t].wait()
    for copy in [head[1], head[0], *tail, time_load, *small[1:]]:
        copy.start()
    for t in (3, 2, 1):
        for r in range(1, rows + 1):
            normalize(lag + t, r)
    def count(condition):
        return jnp.where(condition, 1, 0)

    beside_me = count(has_above) + count(has_below)
    pl.semaphore_wait(barrier, beside_me + count(has_back) * (1 + beside_me))
    greet(has_back, (seq - 1, sp), ready_sem)
    greet(has_back & has_above, (seq - 1, sp - 1), ready_sem)
    greet(has_back & has_below, (seq - 1, sp + 1), ready_sem)

    class Send:
        def __init__(self, slot, source, target, device, leaves, comes):
            self.copy = pltpu.make_async_remote_copy(
                src_ref=source, dst_ref=target,
                send_sem=send_sem.at[slot], recv_sem=recv_sem.at[slot],
                device_id=device, device_id_type=MESH,
            )
            self.leaves, self.comes = leaves, comes
            pl.when(leaves)(self.copy.start)

            @pl.when(jnp.logical_not(comes))
            def _():
                target[...] = jnp.zeros(target.shape, target.dtype)

        def wait_recv(self):
            pl.when(self.comes)(self.copy.wait_recv)

        def wait_send(self):
            pl.when(self.leaves)(self.copy.wait_send)

    last = pl.ds(frames - lag, lag)
    past = pl.ds(0, lag)
    up, down = (seq, sp - 1), (seq, sp + 1)

    def edges(slot, first, size):
        here, there = pl.ds(first, size), pl.ds(lag + first, size)
        return [
            Send(
                slot, x_ref.at[here, rows - 1], x_all.at[there, 0], down, has_below, has_above
            ),
            Send(
                slot + 1, x_ref.at[here, 0], x_all.at[there, rows + 1], up, has_above, has_below
            ),
        ]

    middle = edges(6, 1, 3)
    outer = edges(0, 4, 2) + edges(8, 0, 1)
    for t in (5, 4, 0):
        loads[t].wait()
        queue.extend((lag + t, r) for r in range(1, rows + 1))
    head[2].wait()
    conv((5,), inner, 0, 1, rate=1, only=(2,))

    @pl.when(has_next)
    def _():
        pl.semaphore_wait(ready_sem, 1 + beside_me)

    earlier = [
        Send(
            2, x_ref.at[last], x_all.at[past, pl.ds(1, rows)], (seq + 1, sp), has_next, has_back
        ),
        Send(
            3, x_ref.at[last, rows - 1], x_all.at[past, 0], (seq + 1, sp + 1),
            has_next & has_below, has_back & has_above,
        ),
        Send(
            4, x_ref.at[last, 0], x_all.at[past, rows + 1], (seq + 1, sp - 1),
            has_next & has_above, has_back & has_below,
        ),
    ]
    for s in (4, 3):
        conv((s,), inner, 0, 1, rate=1, only=(2,))
    head[1].wait()
    head[0].wait()
    for s in (5, 4, 3):
        conv((s,), inner, 0, 1, rate=1, only=(0, 1))
    for copy in tail + small[1:]:
        copy.wait()
    for s in (5, 4):
        conv((s,), inner, 1, 2, rate=1)
    for copy in middle:
        copy.wait_recv()
    queue[:0] = [(s, r) for s in (5, 4, 3) for r in (0, rows + 1)]
    conv((3,), inner, 1, 2, rate=2)
    for copy in outer:
        copy.wait_recv()
    queue[:0] = [(s, r) for s in (7, 6) for r in (0, rows + 1)]
    queue.extend((2, r) for r in (0, rows + 1))
    conv((5, 4, 3), edge, rate=2)
    finish(3, total[3])
    beside(len([item for item in queue if item[0] > 2]))
    conv((7,), whole)
    conv((6,), whole, final=(5, 4))
    before_copy = Send(5, resid.at[frames], before, (seq + 1, sp), has_next, has_back)
    time_load.wait()
    outs = [project(2)]
    opening = jnp.int32(0)
    start = jnp.int32(0)
    for j in range(clips.shape[0]):
        opening = opening + jnp.where(start == seq, 1, 0)
        start = start + clips[j]
    keep = (1 - opening).astype(F32)
    beside(len(queue))

    def take_past():
        for copy in earlier:
            copy.wait_recv()
        queue.extend((s, r, keep) for s in reversed(range(lag)) for r in range(rows + 2))

    conv((2,), whole, final=(2,), rate=6, midway=take_past)
    beside(len(queue))
    conv((1,), whole, final=(1,))
    outs.append(project(1))
    conv((0,), whole, final=(0,))
    before_copy.wait_recv()
    resid[0] = (before[...].astype(F32) * keep).astype(BF16)
    outs.append(project(0))
    for copy in [*middle, *outer, *earlier, before_copy]:
        copy.wait_send()
    for copy in outs:
        copy.wait()


def per_device(frames_in, gain, conv_weight, conv_bias, time_weight, time_bias, clip_lengths):
    frames, rows, cols, width = frames_in.shape
    deep = TAPS * TAPS * width
    lag = TAPS - 1
    anywhere = pl.BlockSpec(memory_space=pl.ANY)
    flops = 2 * frames * rows * cols * width * (TAPS * deep + TAPS * width // 2)
    return pl.pallas_call(
        kernel,
        out_shape=jax.ShapeDtypeStruct((frames // 2, rows, cols, width), BF16),
        in_specs=[anywhere] * 7,
        out_specs=anywhere,
        scratch_shapes=[
            pltpu.VMEM((frames + lag, rows + 2, cols, width), BF16),
            pltpu.VMEM((deep, TAPS * width), BF16),
            pltpu.VMEM((TAPS * width, width), BF16),
            pltpu.VMEM((width,), F32),
            pltpu.VMEM((width,), F32),
            pltpu.VMEM((width,), F32),
            pltpu.SMEM(clip_lengths.shape, jnp.int32),
            pltpu.VMEM((frames + lag, rows + 2, cols, TAPS * width), BF16),
            pltpu.VMEM((frames, rows, cols, width), F32),
            pltpu.VMEM((frames + 1, rows * cols, width), BF16),
            pltpu.VMEM((rows * cols, width), BF16),
            pltpu.VMEM((frames // 2, rows, cols, width), BF16),
            pltpu.SemaphoreType.DMA((frames,)),
            pltpu.SemaphoreType.DMA((2 * TAPS + 1,)),
            pltpu.SemaphoreType.DMA((4,)),
            pltpu.SemaphoreType.DMA((10,)),
            pltpu.SemaphoreType.DMA((10,)),
            pltpu.SemaphoreType.DMA((frames // 2,)),
            pltpu.SemaphoreType.REGULAR,
        ],
        compiler_params=pltpu.CompilerParams(
            collective_id=0, has_side_effects=True, vmem_limit_bytes=56 * 2**20
        ),
        cost_estimate=pl.CostEstimate(flops=flops, bytes_accessed=12_000_000, transcendentals=0),
        name="residual_block",
    )(
        frames_in,
        gain,
        conv_weight.reshape(TAPS, deep, width),
        conv_bias,
        time_weight.reshape(TAPS * width, width),
        time_bias,
        clip_lengths,
    )


def solution(mesh):
    return jax.shard_map(
        per_device,
        mesh=mesh,
        in_specs=(P("seq", "sp", None, None), P(), P(), P(), P(), P(), P()),
        out_specs=P("seq", "sp", None, None),
        check_vma=False,
    )
```

```python
import jax
import jax.numpy as jnp
from jax import lax
from jax.experimental import pallas as pl
from jax.experimental.pallas import tpu as pltpu
from jax.sharding import PartitionSpec as P

F32 = jnp.float32
BF16 = jnp.bfloat16
MESH = pl.DeviceIdType.MESH
TAPS = 3
PIECE = 256


def kernel(
    x_ref, gain_ref, cw_ref, cb_ref, tw_ref, tb_ref, clips_ref, out_ref,
    x_all, weight, time_w, gain_v, cb_v, tb_v, clips, joined, total, resid, before, latent,
    x_sem, w_sem, small_sem, send_sem, recv_sem, out_sem, ready_sem,
):
    frames, rows, cols, width = x_ref.shape
    lag = TAPS - 1
    deep = TAPS * width
    seq_count, sp_count = lax.axis_size("seq"), lax.axis_size("sp")
    seq, sp = lax.axis_index("seq"), lax.axis_index("sp")
    has_back, has_next = seq > 0, seq < seq_count - 1
    has_above, has_below = sp > 0, sp < sp_count - 1

    barrier = pltpu.get_barrier_semaphore()

    def greet(condition, device, semaphore=barrier):
        @pl.when(condition)
        def _():
            pl.semaphore_signal(semaphore, inc=1, device_id=device, device_id_type=MESH)

    greet(has_above, (seq, sp - 1))
    greet(has_below, (seq, sp + 1))
    greet(has_next, (seq + 1, sp))
    greet(has_next & has_above, (seq + 1, sp - 1))
    greet(has_next & has_below, (seq + 1, sp + 1))

    small = [
        pltpu.make_async_copy(source, target, small_sem.at[i])
        for i, (source, target) in enumerate((
                (gain_ref, gain_v), (cb_ref, cb_v), (tb_ref, tb_v), (clips_ref, clips)
            ))
    ]
    loads = [
        pltpu.make_async_copy(x_ref.at[t], x_all.at[lag + t, pl.ds(1, rows)], x_sem.at[t])
        for t in range(frames)
    ]

    def weight_load(slot, first, size):
        return [
            pltpu.make_async_copy(
                cw_ref.at[k, pl.ds(first, size)],
                weight.at[pl.ds(first, size), pl.ds(k * width, width)],
                w_sem.at[slot + k],
            )
            for k in range(TAPS)
        ]

    head, tail = weight_load(0, 0, deep), weight_load(TAPS, deep, 2 * deep)
    time_load = pltpu.make_async_copy(tw_ref, time_w, w_sem.at[2 * TAPS])
    small[0].start()
    for t in (3, 2, 1, 5, 4, 0):
        loads[t].start()
    for copy in head:
        copy.start()

    def count(condition):
        return jnp.where(condition, 1, 0)

    beside_me = count(has_above) + count(has_below)
    pl.semaphore_wait(barrier, beside_me + count(has_back) * (1 + beside_me))
    greet(has_back, (seq - 1, sp), ready_sem)
    greet(has_back & has_above, (seq - 1, sp - 1), ready_sem)
    greet(has_back & has_below, (seq - 1, sp + 1), ready_sem)

    class Send:
        def __init__(self, slot, source, target, device, leaves, comes):
            self.copy = pltpu.make_async_remote_copy(
                src_ref=source, dst_ref=target,
                send_sem=send_sem.at[slot], recv_sem=recv_sem.at[slot],
                device_id=device, device_id_type=MESH,
            )
            self.leaves, self.comes = leaves, comes
            pl.when(leaves)(self.copy.start)

            @pl.when(jnp.logical_not(comes))
            def _():
                target[...] = jnp.zeros(target.shape, target.dtype)

        def wait_recv(self):
            pl.when(self.comes)(self.copy.wait_recv)

        def wait_send(self):
            pl.when(self.leaves)(self.copy.wait_send)

    last = pl.ds(frames - lag, lag)
    past = pl.ds(0, lag)
    up, down = (seq, sp - 1), (seq, sp + 1)

    def edges(slot, first, size):
        here, there = pl.ds(first, size), pl.ds(lag + first, size)
        return [
            Send(
                slot, x_ref.at[here, rows - 1], x_all.at[there, 0], down, has_below, has_above
            ),
            Send(
                slot + 1, x_ref.at[here, 0], x_all.at[there, rows + 1], up, has_above, has_below
            ),
        ]

    middle = edges(6, 1, 3)
    outer = edges(0, 4, 2) + edges(8, 0, 1)

    small[0].wait()
    half_gain = gain_v[...].reshape(1, width) * 0.5
    column = lax.broadcasted_iota(jnp.int32, (cols, width), 0)

    def normalize(s, r, factor=None):
        values = x_all[s, r].astype(F32)
        scale = lax.rsqrt(jnp.mean(values * values, axis=-1, keepdims=True) + 1e-06)
        if factor is not None:
            scale = scale * factor
        half = values * scale * half_gain
        act = half + half * jnp.tanh(half)
        joined[s, r, :, pl.ds(width, width)] = act.astype(BF16)
        ahead = jnp.where(column == 0, 0.0, pltpu.roll(act, 1, 0))
        joined[s, r, :, pl.ds(0, width)] = ahead.astype(BF16)
        behind = jnp.where(column == cols - 1, 0.0, pltpu.roll(act, cols - 1, 0))
        joined[s, r, :, pl.ds(2 * width, width)] = behind.astype(BF16)

    queue = []

    def beside(count):
        for _ in range(min(count, len(queue))):
            normalize(*queue.pop(0))

    seen = set()
    inner, edge, whole = (1, rows - 1), None, (0, rows)

    def rows_of(s, part, d):
        if part is edge:
            pair = [joined[s, d], joined[s, rows - 1 + d]]
            return jnp.concatenate(pair, 0)
        lo, hi = part
        return joined[s, lo + d : hi + d].reshape((hi - lo) * cols, deep)

    def conv(sources, part, first=0, count=TAPS, final=(), rate=0, midway=lambda: None):
        left = jnp.concatenate(
            [
                jnp.concatenate([rows_of(s, part, d) for s in sources], 0)
                for d in range(first, first + count)
            ],
            1,
        )
        taps = [k for k in range(TAPS) if 0 <= sources[0] - k < frames]
        deepest, stop = slice(first * deep, (first + count) * deep), (taps[-1] + 1) * width
        pieces = []
        for column in range(taps[0] * width, stop, PIECE):
            columns = slice(column, min(column + PIECE, stop))
            pieces.append(jnp.dot(left, weight[deepest, columns], preferred_element_type=F32))
            if column == taps[0] * width + 2 * PIECE:
                midway()
            beside(rate)
        product = jnp.concatenate(pieces, 1)
        size = left.shape[0] // len(sources)
        sums = {}
        for i, s in enumerate(sources):
            for n, k in enumerate(taps):
                piece = product[i * size : (i + 1) * size, n * width : (n + 1) * width]
                sums[s - k] = sums[s - k] + piece if s - k in sums else piece
        for t, piece in sums.items():
            spots = [0, rows - 1] if part is edge else [slice(*part)]
            for i, spot in enumerate(spots):
                share = piece.shape[0] // len(spots)
                value = piece[i * share : (i + 1) * share]
                value = value.reshape(((share // cols,) if part is not edge else ()) + (cols, width))
                marks = [(t, r) for r in (range(*part) if part is not edge else [spot])]
                if marks[0] in seen:
                    value = total[t, spot] + value
                seen.update(marks)
                if t in final:
                    finish(t, value)
                else:
                    total[t, spot] = value

    def finish(t, summed):
        values = x_all[lag + t, 1 : rows + 1].astype(F32)
        done = values + summed + cb_v[...].reshape(1, 1, width)
        resid[t + 1] = done.reshape(rows * cols, width).astype(BF16)

    def project(j):
        left = jnp.concatenate([resid[2 * j + k] for k in range(TAPS)], 1)
        done = jnp.dot(left, time_w[...], preferred_element_type=F32) + tb_v[...].reshape(1, width)
        latent[j] = done.reshape(rows, cols, width).astype(BF16)
        copy = pltpu.make_async_copy(latent.at[j], out_ref.at[j], out_sem.at[j])
        copy.start()
        return copy

    for t in (3, 2, 1):
        loads[t].wait()
    for copy in tail + [time_load] + small[1:]:
        copy.start()
    for t in (3, 2, 1):
        for r in range(1, rows + 1):
            normalize(lag + t, r)
    for t in (5, 4, 0):
        loads[t].wait()
        queue.extend((lag + t, r) for r in range(1, rows + 1))
    for copy in head:
        copy.wait()
    for s in (5, 4, 3):
        conv((s,), inner, 0, 1, rate=1)

    @pl.when(has_next)
    def _():
        pl.semaphore_wait(ready_sem, 1 + beside_me)

    earlier = [
        Send(
            2, x_ref.at[last], x_all.at[past, pl.ds(1, rows)], (seq + 1, sp), has_next, has_back
        ),
        Send(
            3, x_ref.at[last, rows - 1], x_all.at[past, 0], (seq + 1, sp + 1),
            has_next & has_below, has_back & has_above,
        ),
        Send(
            4, x_ref.at[last, 0], x_all.at[past, rows + 1], (seq + 1, sp - 1),
            has_next & has_above, has_back & has_below,
        ),
    ]
    for copy in tail + small[1:]:
        copy.wait()
    for s in (5, 4):
        conv((s,), inner, 1, 2, rate=1)
    for copy in middle:
        copy.wait_recv()
    queue[:0] = [(s, r) for s in (5, 4, 3) for r in (0, rows + 1)]
    conv((3,), inner, 1, 2, rate=2)
    for copy in outer:
        copy.wait_recv()
    queue[:0] = [(s, r) for s in (7, 6) for r in (0, rows + 1)]
    queue.extend((2, r) for r in (0, rows + 1))
    conv((5, 4, 3), edge, rate=2)
    finish(3, total[3])
    beside(len([item for item in queue if item[0] > 2]))
    conv((7,), whole)
    conv((6,), whole, final=(5, 4))
    before_copy = Send(5, resid.at[frames], before, (seq + 1, sp), has_next, has_back)
    time_load.wait()
    outs = [project(2)]
    opening = jnp.int32(0)
    start = jnp.int32(0)
    for j in range(clips.shape[0]):
        opening = opening + jnp.where(start == seq, 1, 0)
        start = start + clips[j]
    keep = (1 - opening).astype(F32)
    beside(len(queue))

    def take_past():
        for copy in earlier:
            copy.wait_recv()
        queue.extend((s, r, keep) for s in reversed(range(lag)) for r in range(rows + 2))

    conv((2,), whole, final=(2,), rate=6, midway=take_past)
    beside(len(queue))
    conv((1,), whole, final=(1,))
    outs.append(project(1))
    conv((0,), whole, final=(0,))
    before_copy.wait_recv()
    resid[0] = (before[...].astype(F32) * keep).astype(BF16)
    outs.append(project(0))
    for copy in [*middle, *outer, *earlier, before_copy]:
        copy.wait_send()
    for copy in outs:
        copy.wait()


def per_device(frames_in, gain, conv_weight, conv_bias, time_weight, time_bias, clip_lengths):
    frames, rows, cols, width = frames_in.shape
    deep = TAPS * TAPS * width
    lag = TAPS - 1
    anywhere = pl.BlockSpec(memory_space=pl.ANY)
    flops = 2 * frames * rows * cols * width * (TAPS * deep + TAPS * width // 2)
    return pl.pallas_call(
        kernel,
        out_shape=jax.ShapeDtypeStruct((frames // 2, rows, cols, width), BF16),
        in_specs=[anywhere] * 7,
        out_specs=anywhere,
        scratch_shapes=[
            pltpu.VMEM((frames + lag, rows + 2, cols, width), BF16),
            pltpu.VMEM((deep, TAPS * width), BF16),
            pltpu.VMEM((TAPS * width, width), BF16),
            pltpu.VMEM((width,), F32),
            pltpu.VMEM((width,), F32),
            pltpu.VMEM((width,), F32),
            pltpu.SMEM(clip_lengths.shape, jnp.int32),
            pltpu.VMEM((frames + lag, rows + 2, cols, TAPS * width), BF16),
            pltpu.VMEM((frames, rows, cols, width), F32),
            pltpu.VMEM((frames + 1, rows * cols, width), BF16),
            pltpu.VMEM((rows * cols, width), BF16),
            pltpu.VMEM((frames // 2, rows, cols, width), BF16),
            pltpu.SemaphoreType.DMA((frames,)),
            pltpu.SemaphoreType.DMA((2 * TAPS + 1,)),
            pltpu.SemaphoreType.DMA((4,)),
            pltpu.SemaphoreType.DMA((10,)),
            pltpu.SemaphoreType.DMA((10,)),
            pltpu.SemaphoreType.DMA((frames // 2,)),
            pltpu.SemaphoreType.REGULAR,
        ],
        compiler_params=pltpu.CompilerParams(
            collective_id=0, has_side_effects=True, vmem_limit_bytes=56 * 2**20
        ),
        cost_estimate=pl.CostEstimate(flops=flops, bytes_accessed=12_000_000, transcendentals=0),
        name="residual_block",
    )(
        frames_in,
        gain,
        conv_weight.reshape(TAPS, deep, width),
        conv_bias,
        time_weight.reshape(TAPS * width, width),
        time_bias,
        clip_lengths,
    )


def solution(mesh):
    return jax.shard_map(
        per_device,
        mesh=mesh,
        in_specs=(P("seq", "sp", None, None), P(), P(), P(), P(), P(), P()),
        out_specs=P("seq", "sp", None, None),
        check_vma=False,
    )
```

```python
import jax
import jax.numpy as jnp
from jax import lax
from jax.experimental import pallas as pl
from jax.experimental.pallas import tpu as pltpu
from jax.sharding import PartitionSpec as P

F32 = jnp.float32
BF16 = jnp.bfloat16
MESH = pl.DeviceIdType.MESH
TAPS = 3


def kernel(
    x_ref, gain_ref, cw_ref, cb_ref, tw_ref, tb_ref, clips_ref, out_ref,
    x_all, weight, time_w, gain_v, cb_v, tb_v, clips, joined, total, resid, before, latent,
    x_sem, w_sem, small_sem, send_sem, recv_sem, out_sem,
):
    frames, rows, cols, width = x_ref.shape
    lag = TAPS - 1
    deep = TAPS * width
    seq_count, sp_count = lax.axis_size("seq"), lax.axis_size("sp")
    seq, sp = lax.axis_index("seq"), lax.axis_index("sp")
    has_back, has_next = seq > 0, seq < seq_count - 1
    has_above, has_below = sp > 0, sp < sp_count - 1

    barrier = pltpu.get_barrier_semaphore()

    def greet(condition, device):
        @pl.when(condition)
        def _():
            pl.semaphore_signal(barrier, inc=1, device_id=device, device_id_type=MESH)

    greet(has_above, (seq, sp - 1))
    greet(has_below, (seq, sp + 1))
    greet(has_back, (seq - 1, sp))
    greet(has_back & has_above, (seq - 1, sp - 1))
    greet(has_back & has_below, (seq - 1, sp + 1))

    small = [
        pltpu.make_async_copy(source, target, small_sem.at[i])
        for i, (source, target) in enumerate((
                (gain_ref, gain_v), (cb_ref, cb_v), (tb_ref, tb_v), (clips_ref, clips)
            ))
    ]
    loads = [
        pltpu.make_async_copy(x_ref.at[t], x_all.at[lag + t, pl.ds(1, rows)], x_sem.at[t])
        for t in range(frames)
    ]

    def weight_load(slot, first, size):
        return [
            pltpu.make_async_copy(
                cw_ref.at[k, pl.ds(first, size)],
                weight.at[pl.ds(first, size), pl.ds(k * width, width)],
                w_sem.at[slot + k],
            )
            for k in range(TAPS)
        ]

    head, tail = weight_load(0, 0, deep), weight_load(TAPS, deep, 2 * deep)
    time_load = pltpu.make_async_copy(tw_ref, time_w, w_sem.at[2 * TAPS])
    small[0].start()
    for t in (3, 2, 1, 5, 4, 0):
        loads[t].start()
    for copy in head:
        copy.start()

    small[0].wait()
    half_gain = gain_v[...].reshape(1, width) * 0.5
    column = lax.broadcasted_iota(jnp.int32, (cols, width), 0)

    def normalize(s, r, factor=None):
        values = x_all[s, r].astype(F32)
        scale = lax.rsqrt(jnp.mean(values * values, axis=-1, keepdims=True) + 1e-06)
        if factor is not None:
            scale = scale * factor
        half = values * scale * half_gain
        act = half + half * jnp.tanh(half)
        joined[s, r, :, pl.ds(width, width)] = act.astype(BF16)
        ahead = jnp.where(column == 0, 0.0, pltpu.roll(act, 1, 0))
        joined[s, r, :, pl.ds(0, width)] = ahead.astype(BF16)
        behind = jnp.where(column == cols - 1, 0.0, pltpu.roll(act, cols - 1, 0))
        joined[s, r, :, pl.ds(2 * width, width)] = behind.astype(BF16)

    queue = []

    def beside(count):
        for _ in range(min(count, len(queue))):
            normalize(*queue.pop(0))

    seen = set()
    inner, edge, whole = (1, rows - 1), None, (0, rows)

    def rows_of(s, part, d):
        if part is edge:
            pair = [joined[s, d], joined[s, rows - 1 + d]]
            return jnp.concatenate(pair, 0)
        lo, hi = part
        return joined[s, lo + d : hi + d].reshape((hi - lo) * cols, deep)

    def conv(sources, part, first=0, count=TAPS, final=(), rate=0):
        left = jnp.concatenate(
            [
                jnp.concatenate([rows_of(s, part, d) for s in sources], 0)
                for d in range(first, first + count)
            ],
            1,
        )
        taps = [k for k in range(TAPS) if 0 <= sources[0] - k < frames]
        deepest, stop = slice(first * deep, (first + count) * deep), (taps[-1] + 1) * width
        columns = slice(taps[0] * width, stop)
        product = jnp.dot(left, weight[deepest, columns], preferred_element_type=F32)
        beside(rate)
        size = left.shape[0] // len(sources)
        sums = {}
        for i, s in enumerate(sources):
            for n, k in enumerate(taps):
                piece = product[i * size : (i + 1) * size, n * width : (n + 1) * width]
                sums[s - k] = sums[s - k] + piece if s - k in sums else piece
        for t, piece in sums.items():
            spots = [0, rows - 1] if part is edge else [slice(*part)]
            for i, spot in enumerate(spots):
                share = piece.shape[0] // len(spots)
                value = piece[i * share : (i + 1) * share]
                value = value.reshape(((share // cols,) if part is not edge else ()) + (cols, width))
                marks = [(t, r) for r in (range(*part) if part is not edge else [spot])]
                if marks[0] in seen:
                    value = total[t, spot] + value
                seen.update(marks)
                if t in final:
                    finish(t, value)
                else:
                    total[t, spot] = value

    def finish(t, summed):
        values = x_all[lag + t, 1 : rows + 1].astype(F32)
        done = values + summed + cb_v[...].reshape(1, 1, width)
        resid[t + 1] = done.reshape(rows * cols, width).astype(BF16)

    def project(j):
        left = jnp.concatenate([resid[2 * j + k] for k in range(TAPS)], 1)
        done = jnp.dot(left, time_w[...], preferred_element_type=F32) + tb_v[...].reshape(1, width)
        latent[j] = done.reshape(rows, cols, width).astype(BF16)
        copy = pltpu.make_async_copy(latent.at[j], out_ref.at[j], out_sem.at[j])
        copy.start()
        return copy

    for t in (3, 2, 1):
        loads[t].wait()
    for copy in tail + [time_load] + small[1:]:
        copy.start()
    for t in (3, 2, 1):
        for r in range(1, rows + 1):
            normalize(lag + t, r)
    for t in (5, 4, 0):
        loads[t].wait()
        queue.extend((lag + t, r) for r in range(1, rows + 1))
    for copy in head:
        copy.wait()
    conv((5,), inner, 0, 1, rate=5)

    def count(condition):
        return jnp.where(condition, 1, 0)

    beside_me = count(has_above) + count(has_below)
    pl.semaphore_wait(barrier, beside_me + count(has_next) * (1 + beside_me))

    class Send:
        def __init__(self, slot, source, target, device, leaves, comes):
            self.copy = pltpu.make_async_remote_copy(
                src_ref=source, dst_ref=target,
                send_sem=send_sem.at[slot], recv_sem=recv_sem.at[slot],
                device_id=device, device_id_type=MESH,
            )
            self.leaves, self.comes = leaves, comes
            pl.when(leaves)(self.copy.start)

            @pl.when(jnp.logical_not(comes))
            def _():
                target[...] = jnp.zeros(target.shape, target.dtype)

        def wait_recv(self):
            pl.when(self.comes)(self.copy.wait_recv)

        def wait_send(self):
            pl.when(self.leaves)(self.copy.wait_send)

    last = pl.ds(frames - lag, lag)
    past = pl.ds(0, lag)
    up, down = (seq, sp - 1), (seq, sp + 1)

    def edges(slot, first, size):
        here, there = pl.ds(first, size), pl.ds(lag + first, size)
        return [
            Send(
                slot, x_ref.at[here, rows - 1], x_all.at[there, 0], down, has_below, has_above
            ),
            Send(
                slot + 1, x_ref.at[here, 0], x_all.at[there, rows + 1], up, has_above, has_below
            ),
        ]

    middle = edges(6, 1, 3)
    outer = edges(0, 4, 2) + edges(8, 0, 1)
    earlier = [
        Send(
            2, x_ref.at[last], x_all.at[past, pl.ds(1, rows)], (seq + 1, sp), has_next, has_back
        ),
        Send(
            3, x_ref.at[last, rows - 1], x_all.at[past, 0], (seq + 1, sp + 1),
            has_next & has_below, has_back & has_above,
        ),
        Send(
            4, x_ref.at[last, 0], x_all.at[past, rows + 1], (seq + 1, sp - 1),
            has_next & has_above, has_back & has_below,
        ),
    ]

    for s in (4, 3):
        conv((s,), inner, 0, 1, rate=5)
    for copy in tail + small[1:]:
        copy.wait()
    for s in (5, 4):
        conv((s,), inner, 1, 2, rate=5)
    for copy in middle:
        copy.wait_recv()
    queue[:0] = [(s, r) for s in (5, 4, 3) for r in (0, rows + 1)]
    conv((3,), inner, 1, 2, rate=10)
    for copy in outer:
        copy.wait_recv()
    queue[:0] = [(s, r) for s in (7, 6) for r in (0, rows + 1)]
    queue.extend((2, r) for r in (0, rows + 1))
    conv((5, 4, 3), edge, rate=10)
    finish(3, total[3])
    beside(len([item for item in queue if item[0] > 2]))
    conv((7,), whole)
    conv((6,), whole, final=(5, 4))
    before_copy = Send(5, resid.at[frames], before, (seq + 1, sp), has_next, has_back)
    time_load.wait()
    outs = [project(2)]
    opening = jnp.int32(0)
    start = jnp.int32(0)
    for j in range(clips.shape[0]):
        opening = opening + jnp.where(start == seq, 1, 0)
        start = start + clips[j]
    keep = (1 - opening).astype(F32)
    beside(len(queue))
    conv((2,), whole, final=(2,))
    for copy in earlier:
        copy.wait_recv()
    for s in reversed(range(lag)):
        for r in range(rows + 2):
            normalize(s, r, keep)
    conv((1,), whole, final=(1,))
    outs.append(project(1))
    conv((0,), whole, final=(0,))
    before_copy.wait_recv()
    resid[0] = (before[...].astype(F32) * keep).astype(BF16)
    outs.append(project(0))
    for copy in [*middle, *outer, *earlier, before_copy]:
        copy.wait_send()
    for copy in outs:
        copy.wait()


def per_device(frames_in, gain, conv_weight, conv_bias, time_weight, time_bias, clip_lengths):
    frames, rows, cols, width = frames_in.shape
    deep = TAPS * TAPS * width
    lag = TAPS - 1
    anywhere = pl.BlockSpec(memory_space=pl.ANY)
    flops = 2 * frames * rows * cols * width * (TAPS * deep + TAPS * width // 2)
    return pl.pallas_call(
        kernel,
        out_shape=jax.ShapeDtypeStruct((frames // 2, rows, cols, width), BF16),
        in_specs=[anywhere] * 7,
        out_specs=anywhere,
        scratch_shapes=[
            pltpu.VMEM((frames + lag, rows + 2, cols, width), BF16),
            pltpu.VMEM((deep, TAPS * width), BF16),
            pltpu.VMEM((TAPS * width, width), BF16),
            pltpu.VMEM((width,), F32),
            pltpu.VMEM((width,), F32),
            pltpu.VMEM((width,), F32),
            pltpu.SMEM(clip_lengths.shape, jnp.int32),
            pltpu.VMEM((frames + lag, rows + 2, cols, TAPS * width), BF16),
            pltpu.VMEM((frames, rows, cols, width), F32),
            pltpu.VMEM((frames + 1, rows * cols, width), BF16),
            pltpu.VMEM((rows * cols, width), BF16),
            pltpu.VMEM((frames // 2, rows, cols, width), BF16),
            pltpu.SemaphoreType.DMA((frames,)),
            pltpu.SemaphoreType.DMA((2 * TAPS + 1,)),
            pltpu.SemaphoreType.DMA((4,)),
            pltpu.SemaphoreType.DMA((10,)),
            pltpu.SemaphoreType.DMA((10,)),
            pltpu.SemaphoreType.DMA((frames // 2,)),
        ],
        compiler_params=pltpu.CompilerParams(
            collective_id=0, has_side_effects=True, vmem_limit_bytes=56 * 2**20
        ),
        cost_estimate=pl.CostEstimate(flops=flops, bytes_accessed=12_000_000, transcendentals=0),
        name="residual_block",
    )(
        frames_in,
        gain,
        conv_weight.reshape(TAPS, deep, width),
        conv_bias,
        time_weight.reshape(TAPS * width, width),
        time_bias,
        clip_lengths,
    )


def solution(mesh):
    return jax.shard_map(
        per_device,
        mesh=mesh,
        in_specs=(P("seq", "sp", None, None), P(), P(), P(), P(), P(), P()),
        out_specs=P("seq", "sp", None, None),
        check_vma=False,
    )
```
